32 devices in a mesh: tm: 16 (over z, x, core), panel: 2 (over y).
Axes of the slice: x: 2, y: 2, z: 4, core: 2. Of those that a mesh axis runs over, the one named last changes fastest.
Arguments:
- transition: bfloat16 [16, 1024, 1024], P('tm', None, 'panel'), may hold values from -1 to 1
- drift: bfloat16 [16, 1024], P('tm'), may hold values from -6 to 6
- spread: bfloat16 [16, 1024, 1024], P('tm', None, 'panel'), may hold values from -1 to 1, as said below
- belief: bfloat16 [16, 1024], P('tm'), may hold values from -6 to 6
- precision: bfloat16 [16, 1024, 1024], P('tm', None, 'panel'), may hold values from -1 to 1, as said below
- probe_hosts: int32 [16, 256], P('tm'), may hold values from 0 to 511
- probe_values: float32 [16, 256], P('tm'), may hold values from -6 to 6
Outputs:
- sum_transition: bfloat16 [16, 1024, 1024], P('tm', None, 'panel')
- sum_drift: bfloat16 [16, 1024], P('tm')
- sum_spread: bfloat16 [16, 1024, 1024], P('tm', None, 'panel')
- sum_belief: bfloat16 [16, 1024], P('tm')
- sum_precision: bfloat16 [16, 1024, 1024], P('tm', None, 'panel')
The draws below stay inside these ranges and needn't reach their ends.
Inputs may be any that keep to these rules, and one draw needn't show every extreme that they name: `spread`: every 1024 x 1024 block is symmetric. `precision`: every 1024 x 1024 block is symmetric.
All inputs are finite; a program needn't handle non-finite values.
Results may differ from the reference program's by a relative error of at most 0.012.
The reference program's roundings to bfloat16 on the way count: a program that leaves them out, or rounds other values in their place, can miss the bound.
Values may be sent and summed in bfloat16 or wider, within the bound.
A program may use at most 64 MiB of HBM per device.

```python
import math
import jax
import jax.numpy as jnp
from jax import lax

D = 1024
HOSTS = 512
NS = 2
LEVELS = 2
PROBES = 256
N_TM = 16


def dense_noise(key, symmetric):
    noise = jnp.clip(jax.random.normal(key, (N_TM, D, D), jnp.float32), -5.0, 5.0)
    if symmetric:
        noise = (noise + jnp.swapaxes(noise, 1, 2)) * math.sqrt(0.5)
    return noise


def identity_mask():
    row_ids = lax.broadcasted_iota(jnp.int32, (D, D), 0)
    col_ids = lax.broadcasted_iota(jnp.int32, (D, D), 1)
    return (row_ids == col_ids).astype(jnp.float32)


def diagonal_block(key, lowest, highest, noise_scale):
    first_key, second_key = jax.random.split(key)
    diag_values = jax.random.uniform(first_key, (N_TM, D, 1), jnp.float32, lowest, highest)
    noise = dense_noise(second_key, True)
    matrix = diag_values * identity_mask() + noise * (noise_scale / math.sqrt(D))
    return jnp.clip(matrix, -0.99, 0.99)


def draw_transition(key, part):
    base = jax.random.fold_in(key, 101)
    keep_key, skew_key, step_key, noise_key = jax.random.split(base, 4)
    offset_keep = jax.random.uniform(keep_key, (N_TM, D, 1), jnp.float32, 0.5, 0.85)
    skew_keep = jax.random.uniform(skew_key, (N_TM, D, 1), jnp.float32, 0.7, 0.95)
    step_length = jax.random.uniform(step_key, (N_TM, D, 1), jnp.float32, 0.3, 0.7)
    row_ids = lax.broadcasted_iota(jnp.int32, (D, D), 0)
    col_ids = lax.broadcasted_iota(jnp.int32, (D, D), 1)
    even_rows = lax.broadcasted_iota(jnp.int32, (D, 1), 0) % 2 == 0
    upper_mask = ((row_ids % 2 == 0) & (col_ids == row_ids + 1)).astype(jnp.float32)
    keep_values = jnp.where(even_rows, offset_keep, skew_keep)
    noise = dense_noise(noise_key, False)
    matrix = keep_values * identity_mask() + offset_keep * step_length * upper_mask + noise * (0.25 / math.sqrt(D))
    return jnp.clip(matrix, -0.99, 0.99).astype(jnp.bfloat16)


def draw_spread(key, part):
    return diagonal_block(jax.random.fold_in(key, 202), 0.5, 0.85, 0.15).astype(jnp.bfloat16)


def draw_precision(key, part):
    return diagonal_block(jax.random.fold_in(key, 303), 0.45, 0.8, 0.13).astype(jnp.bfloat16)


def plant(result, own_key, low, high):
    spot = [jax.random.randint(jax.random.fold_in(own_key, axis), (), 0, length) for axis, length in enumerate(result.shape)]
    longest = result.shape.index(max(result.shape))
    beside = spot[:longest] + [(spot[longest] + 1) % result.shape[longest]] + spot[longest + 1:]
    return result.at[tuple(spot)].set(low).at[tuple(beside)].set(high)


def levels(stream_key, dims, cuts, least, largest):
    loudness, own = 1.0, jax.random.fold_in(stream_key, 6)
    for position, parts in cuts:
        draws = jnp.exp(jax.random.uniform(jax.random.fold_in(own, position), (parts,), jnp.float32, least / len(cuts), largest / len(cuts)))
        loudness = loudness * jnp.repeat(draws, dims[position] // parts).reshape([-1 if axis == position else 1 for axis in range(len(dims))])
    return loudness


def bell_draw(own_key, shape, scale, most, cuts=(), held_as=jnp.bfloat16):
    entries = scale * jax.random.normal(own_key, shape, jnp.float32)
    if cuts:
        entries = entries * levels(own_key, shape, cuts, -0.22, 0.18)
    return jnp.clip(entries, -most, most).astype(held_as)


def setup_inputs(seed: int = 0) -> dict:
    arg_keys = jax.random.split(jax.random.key(seed), 8)
    transition = draw_transition(jax.random.fold_in(arg_keys[7], 71), 0)
    drift = bell_draw(arg_keys[1], (N_TM, D), 1.0, 6.0, ((0, 16),))
    spread = draw_spread(jax.random.fold_in(arg_keys[7], 71), 0)
    belief = bell_draw(arg_keys[3], (N_TM, D), 1.0, 6.0, ((0, 16),))
    precision = draw_precision(jax.random.fold_in(arg_keys[7], 71), 0)
    probe_hosts = plant(jax.random.randint(arg_keys[5], (N_TM, PROBES), 0, HOSTS), jax.random.fold_in(arg_keys[5], 1), 0, HOSTS - 1).astype(jnp.int32)
    probe_values = bell_draw(arg_keys[6], (N_TM, PROBES), 1.0, 6.0, ((0, 16),), jnp.float32)
    return dict(transition=transition, drift=drift, spread=spread, belief=belief, precision=precision, probe_hosts=probe_hosts, probe_values=probe_values)


def mat_vector(matrix, vector):
    return jnp.dot(matrix, vector.astype(jnp.bfloat16), preferred_element_type=jnp.float32)


def tmat_vector(matrix, vector):
    return jnp.dot(vector.astype(jnp.bfloat16), matrix, preferred_element_type=jnp.float32)


def series_panel(cov_full, info_full, anchor, series_terms):
    current = anchor
    for repeat in range(series_terms):
        inside = jnp.dot(info_full, current, preferred_element_type=jnp.float32).astype(jnp.bfloat16)
        outside = jnp.dot(cov_full, inside, preferred_element_type=jnp.float32)
        current = (anchor.astype(jnp.float32) - outside).astype(jnp.bfloat16)
    return current


def series_forward(cov_full, info_full, anchor, series_terms):
    current = anchor
    for repeat in range(series_terms):
        current = anchor - mat_vector(cov_full, mat_vector(info_full, current))
    return current


def series_backward(cov_full, info_full, anchor, series_terms):
    current = anchor
    for repeat in range(series_terms):
        current = anchor - mat_vector(info_full, mat_vector(cov_full, current))
    return current


def combine(earlier, latter):
    move_early, drift_early, spread_early, belief_early, weight_early = earlier
    move_late, drift_late, spread_late, belief_late, weight_late = latter
    series_terms = 2 ** NS - 1
    crossed = lax.dot_general(spread_early, move_late, (((1,), (1,)), ((), ())), preferred_element_type=jnp.float32).astype(jnp.bfloat16)
    carried = series_panel(spread_early, weight_late, move_early, series_terms)
    widened = series_panel(spread_early, weight_late, crossed, series_terms)
    move_new = jnp.dot(move_late, carried, preferred_element_type=jnp.float32).astype(jnp.bfloat16)
    spread_new = (jnp.dot(move_late, widened, preferred_element_type=jnp.float32) + spread_late.astype(jnp.float32)).astype(jnp.bfloat16)
    weighted = jnp.dot(weight_late, carried, preferred_element_type=jnp.float32).astype(jnp.bfloat16)
    weight_new = (lax.dot_general(move_early, weighted, (((0,), (0,)), ((), ())), preferred_element_type=jnp.float32) + weight_early.astype(jnp.float32)).astype(jnp.bfloat16)
    forward = drift_early.astype(jnp.float32) + mat_vector(spread_early, belief_late)
    forward = series_forward(spread_early, weight_late, forward, series_terms)
    drift_new = (mat_vector(move_late, forward) + drift_late.astype(jnp.float32)).astype(jnp.bfloat16)
    backward = belief_late.astype(jnp.float32) - mat_vector(weight_late, drift_early)
    backward = series_backward(spread_early, weight_late, backward, series_terms)
    belief_new = (tmat_vector(move_early, backward) + belief_early.astype(jnp.float32)).astype(jnp.bfloat16)
    return move_new, drift_new, spread_new, belief_new, weight_new


def combine_matched(matched):
    return combine(matched[0], matched[1])


def reference(transition, drift, spread, belief, precision, probe_hosts, probe_values):
    slab_rows = jnp.arange(N_TM, dtype=jnp.int32)[:, None] * jnp.ones_like(probe_hosts)
    offsets = jnp.zeros((N_TM, HOSTS), jnp.float32).at[slab_rows, probe_hosts].add(probe_values)
    paired = jnp.stack([offsets, jnp.zeros_like(offsets)], axis=2).reshape(N_TM, D)
    belief_start = (belief.astype(jnp.float32) + paired).astype(jnp.bfloat16)
    elements = (transition, drift, spread, belief_start, precision)
    for height in range(LEVELS):
        earlier = tuple(member[0::2] for member in elements)
        latter = tuple(member[1::2] for member in elements)
        elements = lax.map(combine_matched, (earlier, latter))
    copies = 2 ** LEVELS
    outcome = tuple(jnp.repeat(member, copies, axis=0) for member in elements)
    return outcome[0], outcome[1], outcome[2], outcome[3], outcome[4]
```

```python
import functools

import jax
import jax.numpy as jnp
from jax import lax
from jax.experimental import pallas as pl
from jax.experimental.pallas import tpu as pltpu
from jax.sharding import PartitionSpec as P

NS = 2
TERMS = 2**NS - 1
F32 = jnp.float32
BF16 = jnp.bfloat16
MESH = pl.DeviceIdType.MESH
NN = (((1,), (0,)), ((), ()))
NT = (((1,), (1,)), ((), ()))
TN = (((0,), (0,)), ((), ()))


def dot(lhs, rhs, dims=NN):
    return lax.dot_general(lhs, rhs, dims, preferred_element_type=F32)


def kernel(
    panels, names,
    a_ref, c_ref, j_ref, b_ref, eta_ref, hosts_ref, values_ref,
    a_out, c_out, j_out, vec_out,
    s0, a0, s1, a1, v0, v1, anchor, cur, inner, weighted, send_sem, recv_sem,
):
    states, width = a_ref.shape
    tile = min(width, 256)
    tiles = width // tile
    time = lax.axis_index("tm")
    me = lax.axis_index("panel")
    core = lax.rem(time, 2)
    half = lax.rem(lax.div(time, 2), 2)
    core_peer = time + 1 - 2 * core
    side_peer = time + 2 - 4 * half
    cross_peer = core_peer + 2 - 4 * half
    own_cols = pl.ds(pl.multiple_of(me * width, width), width)

    def sem(name):
        return names.setdefault(name, len(names))

    def copy(name, src, dst, at, panel=None):
        index = sem(name)
        return pltpu.make_async_remote_copy(
            src_ref=src, dst_ref=dst,
            send_sem=send_sem.at[index], recv_sem=recv_sem.at[index],
            device_id=(at, me if panel is None else panel), device_id_type=MESH,
        )

    def panel_block(ref, slot, rows, cols):
        return ref.at[slot, rows, cols]

    def chunk_rows(target, chunk):
        if panels != 2:
            return pl.ds(0, states)
        block = lax.rem(target + chunk, 2)
        return pl.ds(pl.multiple_of(block * width, width), width)

    def cols_of(panel):
        return pl.ds(pl.multiple_of(panel * width, width), width)

    def across(name, ref, slot, step, chunk):
        target = lax.rem(me + step, panels)
        block = panel_block(ref, slot, chunk_rows(target, chunk), own_cols)
        return copy(f"{name}y{step}.{chunk}", block, block, time, target)

    def onward(name, ref, slot, step, chunk):
        source = lax.rem(me - step + panels, panels)
        block = panel_block(ref, slot, chunk_rows(me, chunk), cols_of(source))
        return copy(f"{name}f{step}.{chunk}", block, block, core_peer)

    def beside(name, ref, slot):
        block = ref.at[slot, :, own_cols]
        return copy(f"{name}c", block, block, core_peer)

    def sideways(name, ref, slot):
        block = ref.at[slot, :, own_cols]
        return copy(f"{name}x", block, block, side_peer)

    steps = range(1, panels)
    sym_chunks = (1,) if panels == 2 else (0,)
    all_chunks = (0, 1) if panels == 2 else (0,)

    def products(lhs, rhs, dims, put):
        @pl.loop(0, tiles)
        def _(index):
            cols = pl.ds(pl.multiple_of(index * tile, tile), tile)
            put(cols, dot(lhs[...], rhs(cols), dims))

    def into(ref):
        def put(cols, value):
            ref[:, cols] = value.astype(BF16)
        return put

    def series(cov, info):
        cur[...] = anchor[...]

        @pl.loop(0, TERMS)
        def _(repeat):
            products(info, lambda cols: cur[:, cols], NN, into(inner))

            def put(cols, value):
                cur[:, cols] = (anchor[:, cols].astype(F32) - value).astype(BF16)

            products(cov, lambda cols: inner[:, cols], NN, put)

    def vec_series(start, first, second):
        def step(repeat, vector):
            middle = dot(vector.astype(BF16), first[...])
            return start - dot(middle.astype(BF16), second[...])

        return lax.fori_loop(0, TERMS, step, start)

    def mirror(ref, slot):
        if panels == 2:
            other = pl.ds(pl.multiple_of((1 - me) * width, width), width)
            ref[slot, own_cols, other] = ref[slot, other, own_cols].T

    def start_sym(name, ref, slot):
        for step in steps:
            for chunk in sym_chunks:
                across(name, ref, slot, step, chunk).start()
        beside(name, ref, slot).start()

    def start_moves(name, ref, slot):
        for step in steps:
            for chunk in all_chunks:
                across(name, ref, slot, step, chunk).start()

    def gather_sym(name, ref, slot):
        for step in steps:
            for chunk in sym_chunks:
                across(name, ref, slot, step, chunk).wait_recv()
                onward(name, ref, slot, step, chunk).start()
        beside(name, ref, slot).wait_recv()
        for step in steps:
            for chunk in sym_chunks:
                onward(name, ref, slot, step, chunk).wait_recv()
        mirror(ref, 0)
        mirror(ref, 1)

    def end_sends(name, ref, slot):
        for step in steps:
            for chunk in sym_chunks:
                across(name, ref, slot, step, chunk).wait_send()
                onward(name, ref, slot, step, chunk).wait_send()
        beside(name, ref, slot).wait_send()

    barrier = pltpu.get_barrier_semaphore()
    for at in (core_peer, side_peer, cross_peer):
        pl.semaphore_signal(barrier, inc=1, device_id=(at, me), device_id_type=MESH)
    for step in steps:
        pl.semaphore_signal(
            barrier, inc=1, device_id=(time, lax.rem(me + step, panels)), device_id_type=MESH
        )
    pl.semaphore_wait(barrier, 3 + len(steps))

    @pl.when(core == 0)
    def _():
        s0[0, :, own_cols] = c_ref[...]

    @pl.when(core == 1)
    def _():
        s0[1, :, own_cols] = j_ref[...]

    start_sym("s0", s0, core)
    a0[core, :, own_cols] = a_ref[...]
    start_moves("a0", a0, core)

    @pl.when(core == 1)
    def _():
        beside("a0", a0, 1).start()

    hosts = jnp.broadcast_to(hosts_ref[...].astype(F32) * 2.0, (8, hosts_ref.shape[1])).T[:, :1]
    values = jnp.broadcast_to(values_ref[...], (8, values_ref.shape[1])).T[:, :1]
    spots = lax.broadcasted_iota(jnp.int32, (hosts.shape[0], states), 1).astype(F32)
    paired = jnp.sum(jnp.where(hosts == spots, values, 0.0), axis=0, keepdims=True)
    belief = (eta_ref[...].astype(F32) + paired).astype(BF16).astype(F32)
    v0[core, 0] = jnp.broadcast_to(b_ref[...].astype(F32), (16, states))
    v0[core, 1] = jnp.broadcast_to(belief, (16, states))

    def vec0():
        return copy("v0", v0.at[core], v0.at[core], core_peer)

    vec0().start()
    gather_sym("s0", s0, core)
    vec0().wait_recv()

    def vec1(kind, at, tag):
        block = v1.at[half, kind]
        return copy(f"v1{kind}{tag}", block, block, at)

    vec1_peers = ((core_peer, "c"), (side_peer, "x"), (cross_peer, "d"))

    def late_part(name, cov, info, moves, vecs, addend, store):
        for step in steps:
            across(name, moves, 1, step, 0).wait_recv()
            onward(name, moves, 1, step, 0).start()
        own_rows = me * width

        def rows(cols):
            return moves[1, pl.ds(pl.multiple_of(own_rows + cols.start, tile), tile), :]

        products(cov, rows, NT, into(anchor))
        series(cov, info)
        start = vecs[0, 0] + dot(vecs[1, 1].astype(BF16), cov[...])
        forward = vec_series(start, info, cov)
        for step in steps:
            for chunk in all_chunks[1:]:
                across(name, moves, 1, step, chunk).wait_recv()
                onward(name, moves, 1, step, chunk).start()

        def put(cols, value):
            store(cols, (value + addend(cols).astype(F32)).astype(BF16))

        products(moves.at[1], lambda cols: cur[:, cols], NN, put)
        fresh = dot(forward.astype(BF16), moves[1], NT) + vecs[1, 0]
        return fresh.astype(BF16).astype(F32)

    def early_part(name, cov, info, moves, vecs, addend, store_info, sent_info, store_move):
        anchor[...] = moves[0, :, own_cols]
        series(cov, info)
        products(info, lambda cols: cur[:, cols], NN, into(weighted))
        start = vecs[1, 1] - dot(vecs[0, 0].astype(BF16), info[...])
        backward = vec_series(start, cov, info)
        for step in steps:
            for chunk in all_chunks:
                across(name, moves, 0, step, chunk).wait_recv()

        def put(cols, value):
            store_info(cols, (value + addend(cols).astype(F32)).astype(BF16))

        products(moves.at[0], lambda cols: weighted[:, cols], TN, put)
        sent_info()
        fresh = dot(backward.astype(BF16), moves[0]) + vecs[0, 1]
        if name == "a0":
            beside(name, moves, 1).wait_recv()
        for step in steps:
            for chunk in all_chunks:
                onward(name, moves, 1, step, chunk).wait_recv()
        products(moves.at[1], lambda cols: cur[:, cols], NN, store_move)
        return fresh.astype(BF16).astype(F32)

    info_slot = 2 - half
    cov_slot = 3 * half

    def wide(cols):
        return pl.ds(pl.multiple_of(me * width + cols.start, tile), tile)

    def share_vec(kind, value):
        v1[half, kind] = value
        for at, tag in vec1_peers:
            vec1(kind, at, tag).start()

    @pl.when(core == 0)
    def _():
        def store_info(cols, value):
            s1[info_slot, :, wide(cols)] = value

        def store_move(cols, value):
            a1[half, :, wide(cols)] = value.astype(BF16)

        def sent_info():
            @pl.when(half == 1)
            def _():
                sideways("j1", s1, info_slot).start()
                start_sym("s1", s1, 1)

        fresh = early_part(
            "a0", s0.at[0], s0.at[1], a0, v0, lambda cols: j_ref[:, cols],
            store_info, sent_info, store_move,
        )
        sideways("a1", a1, half).start()
        share_vec(1, fresh)

        @pl.when(half == 0)
        def _():
            start_moves("a1", a1, 0)
            sideways("j1", s1, info_slot).start()
            sideways("j1", s1, 1).wait_recv()
            start_sym("s1", s1, 1)
            sideways("a1", a1, 1).wait_recv()
            beside("a1", a1, 1).start()

        @pl.when(half == 1)
        def _():
            beside("a1", a1, 1).start()
            sideways("a1", a1, 0).wait_recv()
            start_moves("a1", a1, 0)

        gather_sym("s1", s1, 1)
        for kind, at, tag in ((0, core_peer, "c"), (1, side_peer, "x"), (0, cross_peer, "d")):
            vec1(kind, at, tag).wait_recv()

        @pl.when(half == 1)
        def _():
            sideways("j1", s1, 2).wait_recv()

        def put_info(cols, value):
            j_out[:, cols] = value

        def send_info():
            copy("jo", j_out, j_out, core_peer).start()

        fresh = early_part(
            "a1", s1.at[0], s1.at[1], a1, v1, lambda cols: s1[2, :, wide(cols)],
            put_info, send_info, into(a_out),
        )
        copy("ao", a_out, a_out, core_peer).start()
        vec_out[1] = fresh
        copy("eo", vec_out.at[1], vec_out.at[1], core_peer).start()
        copy("co", c_out, c_out, core_peer).wait_recv()
        copy("bo", vec_out.at[0], vec_out.at[0], core_peer).wait_recv()
        for step in steps:
            for chunk in all_chunks:
                across("a0", a0, 0, step, chunk).wait_send()
                across("a1", a1, 0, step, chunk).wait_send()
        end_sends("s1", s1, 1)
        sideways("j1", s1, info_slot).wait_send()
        sideways("a1", a1, half).wait_send()
        beside("a1", a1, 1).wait_send()
        for at, tag in vec1_peers:
            vec1(1, at, tag).wait_send()
        copy("jo", j_out, j_out, core_peer).wait_send()
        copy("ao", a_out, a_out, core_peer).wait_send()
        copy("eo", vec_out.at[1], vec_out.at[1], core_peer).wait_send()

    @pl.when(core == 1)
    def _():
        def store_cov(cols, value):
            s1[cov_slot, :, wide(cols)] = value

        fresh = late_part(
            "a0", s0.at[0], s0.at[1], a0, v0, lambda cols: c_ref[:, cols], store_cov
        )

        @pl.when(half == 0)
        def _():
            sideways("c1", s1, 0).start()
            start_sym("s1", s1, 0)

        share_vec(0, fresh)

        @pl.when(half == 1)
        def _():
            sideways("c1", s1, 0).wait_recv()
            start_sym("s1", s1, 0)

        beside("a1", a1, 1).wait_recv()
        start_moves("a1", a1, 1)

        @pl.when(half == 1)
        def _():
            sideways("c1", s1, 3).start()

        gather_sym("s1", s1, 0)
        for kind, at, tag in ((1, core_peer, "c"), (0, side_peer, "x"), (1, cross_peer, "d")):
            vec1(kind, at, tag).wait_recv()

        @pl.when(half == 0)
        def _():
            sideways("c1", s1, 3).wait_recv()

        def put_cov(cols, value):
            c_out[:, cols] = value

        fresh = late_part(
            "a1", s1.at[0], s1.at[1], a1, v1, lambda cols: s1[3, :, wide(cols)], put_cov
        )
        copy("co", c_out, c_out, core_peer).start()
        vec_out[0] = fresh
        copy("bo", vec_out.at[0], vec_out.at[0], core_peer).start()
        copy("jo", j_out, j_out, core_peer).wait_recv()
        copy("ao", a_out, a_out, core_peer).wait_recv()
        copy("eo", vec_out.at[1], vec_out.at[1], core_peer).wait_recv()
        for step in steps:
            for chunk in all_chunks:
                for name, ref in (("a0", a0), ("a1", a1)):
                    across(name, ref, 1, step, chunk).wait_send()
                    onward(name, ref, 1, step, chunk).wait_send()
        beside("a0", a0, 1).wait_send()
        end_sends("s1", s1, 0)
        sideways("c1", s1, cov_slot).wait_send()
        for at, tag in vec1_peers:
            vec1(0, at, tag).wait_send()
        copy("co", c_out, c_out, core_peer).wait_send()
        copy("bo", vec_out.at[0], vec_out.at[0], core_peer).wait_send()

    end_sends("s0", s0, core)
    vec0().wait_send()


def local(panels, transition, drift, spread, belief, precision, probe_hosts, probe_values):
    states, width = transition.shape[1:]
    panel = jax.ShapeDtypeStruct((states, width), BF16)
    vmem = pl.BlockSpec(memory_space=pltpu.VMEM)
    square = (states, states)
    count = 24 + 16 * (panels - 1)
    combine = 2 * states * states * width
    a, c, j, vecs = pl.pallas_call(
        functools.partial(kernel, panels, {}),
        out_shape=(panel, panel, panel, jax.ShapeDtypeStruct((2, 16, states), F32)),
        in_specs=[vmem] * 7,
        out_specs=(vmem,) * 4,
        scratch_shapes=[
            pltpu.VMEM((2,) + square, BF16),
            pltpu.VMEM((2,) + square, BF16),
            pltpu.VMEM((4,) + square, BF16),
            pltpu.VMEM((2,) + square, BF16),
            pltpu.VMEM((2, 2, 16, states), F32),
            pltpu.VMEM((2, 2, 16, states), F32),
            pltpu.VMEM((states, width), BF16),
            pltpu.VMEM((states, width), BF16),
            pltpu.VMEM((states, width), BF16),
            pltpu.VMEM((states, width), BF16),
            pltpu.SemaphoreType.DMA((count,)),
            pltpu.SemaphoreType.DMA((count,)),
        ],
        compiler_params=pltpu.CompilerParams(
            collective_id=0, has_side_effects=True, vmem_limit_bytes=56 * 2**20
        ),
        cost_estimate=pl.CostEstimate(
            flops=18 * combine, bytes_accessed=12 * states * width, transcendentals=0
        ),
    )(
        transition[0], spread[0], precision[0], drift, belief, probe_hosts, probe_values
    )
    fresh = vecs[:, 0].astype(BF16)
    return a[None], fresh[0:1], c[None], fresh[1:2], j[None]


def solution(mesh):
    matrix = P("tm", None, "panel")
    vector = P("tm", None)
    return jax.shard_map(
        functools.partial(local, mesh.shape["panel"]),
        mesh=mesh,
        in_specs=(matrix, vector, matrix, vector, matrix, vector, vector),
        out_specs=(matrix, vector, matrix, vector, matrix),
        check_vma=False,
    )
```

```python
import functools

import jax
import jax.numpy as jnp
from jax import lax
from jax.experimental import pallas as pl
from jax.experimental.pallas import tpu as pltpu
from jax.sharding import PartitionSpec as P

NS = 2
TERMS = 2**NS - 1
F32 = jnp.float32
BF16 = jnp.bfloat16
MESH = pl.DeviceIdType.MESH
NN = (((1,), (0,)), ((), ()))
NT = (((1,), (1,)), ((), ()))
TN = (((0,), (0,)), ((), ()))


def dot(lhs, rhs, dims=NN):
    return lax.dot_general(lhs, rhs, dims, preferred_element_type=F32)


def kernel(
    panels, names,
    a_ref, c_ref, j_ref, b_ref, eta_ref, hosts_ref, values_ref,
    a_out, c_out, j_out, vec_out,
    s0, a0, s1, a1, v0, v1, anchor, cur, inner, weighted, send_sem, recv_sem,
):
    states, width = a_ref.shape
    tile = min(width, 256)
    tiles = width // tile
    time = lax.axis_index("tm")
    me = lax.axis_index("panel")
    core = lax.rem(time, 2)
    half = lax.rem(lax.div(time, 2), 2)
    core_peer = time + 1 - 2 * core
    side_peer = time + 2 - 4 * half
    cross_peer = core_peer + 2 - 4 * half
    own_cols = pl.ds(pl.multiple_of(me * width, width), width)

    def sem(name):
        return names.setdefault(name, len(names))

    def copy(name, src, dst, at, panel=None):
        index = sem(name)
        return pltpu.make_async_remote_copy(
            src_ref=src, dst_ref=dst,
            send_sem=send_sem.at[index], recv_sem=recv_sem.at[index],
            device_id=(at, me if panel is None else panel), device_id_type=MESH,
        )

    def panel_block(ref, slot, rows, cols):
        return ref.at[slot, rows, cols]

    def chunk_rows(target, chunk):
        if panels != 2:
            return pl.ds(0, states)
        block = lax.rem(target + chunk, 2)
        return pl.ds(pl.multiple_of(block * width, width), width)

    def cols_of(panel):
        return pl.ds(pl.multiple_of(panel * width, width), width)

    def across(name, ref, slot, step, chunk):
        target = lax.rem(me + step, panels)
        block = panel_block(ref, slot, chunk_rows(target, chunk), own_cols)
        return copy(f"{name}y{step}.{chunk}", block, block, time, target)

    def onward(name, ref, slot, step, chunk):
        source = lax.rem(me - step + panels, panels)
        block = panel_block(ref, slot, chunk_rows(me, chunk), cols_of(source))
        return copy(f"{name}f{step}.{chunk}", block, block, core_peer)

    def beside(name, ref, slot, chunk):
        block = panel_block(ref, slot, chunk_rows(me + 1, chunk), own_cols)
        return copy(f"{name}c{chunk}", block, block, core_peer)

    def sideways(name, ref, slot, chunk, at=side_peer):
        block = panel_block(ref, slot, chunk_rows(me + 1, chunk), own_cols)
        return copy(f"{name}x{chunk}", block, block, at)

    steps = range(1, panels)
    sym_chunks = (1,) if panels == 2 else (0,)
    all_chunks = (0, 1) if panels == 2 else (0,)
    sym_first = all_chunks[::-1]

    def products(lhs, rhs, dims, put):
        @pl.loop(0, tiles)
        def _(index):
            cols = pl.ds(pl.multiple_of(index * tile, tile), tile)
            put(cols, dot(lhs[...], rhs(cols), dims))

    def into(ref):
        def put(cols, value):
            ref[:, cols] = value.astype(BF16)
        return put

    def series(cov, info):
        cur[...] = anchor[...]

        @pl.loop(0, TERMS)
        def _(repeat):
            products(info, lambda cols: cur[:, cols], NN, into(inner))

            def put(cols, value):
                cur[:, cols] = (anchor[:, cols].astype(F32) - value).astype(BF16)

            products(cov, lambda cols: inner[:, cols], NN, put)

    def vec_series(start, first, second):
        def step(repeat, vector):
            middle = dot(vector.astype(BF16), first[...])
            return start - dot(middle.astype(BF16), second[...])

        return lax.fori_loop(0, TERMS, step, start)

    def mirror(ref, slot):
        if panels == 2:
            other = pl.ds(pl.multiple_of((1 - me) * width, width), width)
            ref[slot, own_cols, other] = ref[slot, other, own_cols].T

    def start_across(name, ref, slot, chunks):
        for step in steps:
            for chunk in chunks:
                across(name, ref, slot, step, chunk).start()

    def start_beside(name, ref, slot, chunks=sym_first):
        for chunk in chunks:
            beside(name, ref, slot, chunk).start()

    def pass_sym(name, ref, slot):
        for step in steps:
            for chunk in sym_chunks:
                across(name, ref, slot, step, chunk).wait_recv()
                onward(name, ref, slot, step, chunk).start()

    def gather_sym(name, ref, slot):
        for chunk in sym_first:
            beside(name, ref, slot, chunk).wait_recv()
        for step in steps:
            for chunk in sym_chunks:
                onward(name, ref, slot, step, chunk).wait_recv()
        mirror(ref, 0)
        mirror(ref, 1)

    def end_sends(name, ref, slot):
        for step in steps:
            for chunk in sym_chunks:
                if name != "s0":
                    across(name, ref, slot, step, chunk).wait_send()
                onward(name, ref, slot, step, chunk).wait_send()
        for chunk in sym_first:
            beside(name, ref, slot, chunk).wait_send()

    barrier = pltpu.get_barrier_semaphore()
    for at in (core_peer, side_peer, cross_peer):
        pl.semaphore_signal(barrier, inc=1, device_id=(at, me), device_id_type=MESH)
    for step in steps:
        pl.semaphore_signal(
            barrier, inc=1, device_id=(time, lax.rem(me + step, panels)), device_id_type=MESH
        )
    pl.semaphore_wait(barrier, 3 + len(steps))

    @pl.when(core == 0)
    def _():
        s0[0, :, own_cols] = c_ref[...]

    @pl.when(core == 1)
    def _():
        s0[1, :, own_cols] = j_ref[...]

    start_across("s0", s0, core, sym_chunks)
    start_beside("s0", s0, core)
    a0[core, :, own_cols] = a_ref[...]

    @pl.when(core == 1)
    def _():
        start_beside("a0", a0, 1, all_chunks)

    hosts = jnp.broadcast_to(hosts_ref[...].astype(F32) * 2.0, (8, hosts_ref.shape[1])).T[:, :1]
    values = jnp.broadcast_to(values_ref[...], (8, values_ref.shape[1])).T[:, :1]
    spots = lax.broadcasted_iota(jnp.int32, (hosts.shape[0], states), 1).astype(F32)
    paired = jnp.sum(jnp.where(hosts == spots, values, 0.0), axis=0, keepdims=True)
    belief = (eta_ref[...].astype(F32) + paired).astype(BF16).astype(F32)
    v0[core, 0] = jnp.broadcast_to(b_ref[...].astype(F32), (16, states))
    v0[core, 1] = jnp.broadcast_to(belief, (16, states))

    def vec0():
        return copy("v0", v0.at[core], v0.at[core], core_peer)

    vec0().start()
    for step in steps:
        for chunk in sym_chunks:
            across("s0", s0, core, step, chunk).wait_send()
    start_across("a0", a0, core, all_chunks)
    pass_sym("s0", s0, core)
    gather_sym("s0", s0, core)
    vec0().wait_recv()

    def vec1(kind, at, tag):
        block = v1.at[half, kind]
        return copy(f"v1{kind}{tag}", block, block, at)

    vec1_peers = ((core_peer, "c"), (side_peer, "x"), (cross_peer, "d"))

    def late_part(name, cov, info, moves, vecs, addend, ready, store):
        start = vecs[0, 0] + dot(vecs[1, 1].astype(BF16), cov[...])
        forward = vec_series(start, info, cov)
        if name == "a1":
            @pl.when(half == 0)
            def _():
                for chunk in all_chunks:
                    sideways("a1", a1, 1, chunk).wait_recv()
                    start_across("a1", a1, 1, (chunk,))
                    beside("b1", a1, 1, chunk).start()

        for step in steps:
            across(name, moves, 1, step, 0).wait_recv()
            onward(name, moves, 1, step, 0).start()
        own_rows = me * width

        def rows(cols):
            return moves[1, pl.ds(pl.multiple_of(own_rows + cols.start, tile), tile), :]

        products(cov, rows, NT, into(anchor))
        series(cov, info)
        for step in steps:
            for chunk in all_chunks[1:]:
                across(name, moves, 1, step, chunk).wait_recv()
                onward(name, moves, 1, step, chunk).start()

        ready()

        def put(cols, value):
            store(cols, (value + addend(cols).astype(F32)).astype(BF16))

        products(moves.at[1], lambda cols: cur[:, cols], NN, put)
        fresh = dot(forward.astype(BF16), moves[1], NT) + vecs[1, 0]
        return fresh.astype(BF16).astype(F32)

    def early_part(name, cov, info, moves, vecs, addend, ready_info, store_info, sent_info, store_move):
        anchor[...] = moves[0, :, own_cols]
        series(cov, info)
        products(info, lambda cols: cur[:, cols], NN, into(weighted))
        start = vecs[1, 1] - dot(vecs[0, 0].astype(BF16), info[...])
        backward = vec_series(start, cov, info)
        for step in steps:
            for chunk in all_chunks:
                across(name, moves, 0, step, chunk).wait_recv()

        ready_info()

        def put(cols, value):
            store_info(cols, (value + addend(cols).astype(F32)).astype(BF16))

        products(moves.at[0], lambda cols: weighted[:, cols], TN, put)
        sent_info()
        fresh = dot(backward.astype(BF16), moves[0]) + vecs[0, 1]
        if name == "a0":
            for chunk in all_chunks:
                beside(name, moves, 1, chunk).wait_recv()
        else:
            @pl.when(half == 0)
            def _():
                for chunk in all_chunks:
                    beside("b1", moves, 1, chunk).wait_recv()

        for step in steps:
            for chunk in all_chunks:
                onward(name, moves, 1, step, chunk).wait_recv()
        products(moves.at[1], lambda cols: cur[:, cols], NN, store_move)
        return fresh.astype(BF16).astype(F32)

    info_slot = 2 - half
    cov_slot = 3 * half

    def wide(cols):
        return pl.ds(pl.multiple_of(me * width + cols.start, tile), tile)

    def share_vec(kind, value):
        v1[half, kind] = value
        for at, tag in vec1_peers:
            vec1(kind, at, tag).start()

    @pl.when(core == 0)
    def _():
        def store_info(cols, value):
            s1[info_slot, :, wide(cols)] = value

        def store_move(cols, value):
            a1[half, :, wide(cols)] = value.astype(BF16)

        def sent_info():
            @pl.when(half == 1)
            def _():
                sideways("j1", s1, 1, sym_first[0]).start()
                start_across("s1", s1, 1, sym_chunks)
                start_beside("s1", s1, 1)

        fresh = early_part(
            "a0", s0.at[0], s0.at[1], a0, v0, lambda cols: j_ref[:, cols],
            lambda: None, store_info, sent_info, store_move,
        )
        share_vec(1, fresh)

        @pl.when(half == 0)
        def _():
            for chunk in all_chunks:
                sideways("a1", a1, 0, chunk).start()
            start_across("a1", a1, 0, all_chunks[:1])
            sideways("j1", s1, 1, sym_first[0]).wait_recv()
            start_across("s1", s1, 1, sym_chunks)
            start_beside("s1", s1, 1, sym_first[:1])

        @pl.when(half == 1)
        def _():
            start_beside("a1", a1, 1, all_chunks)
            sideways("j1", s1, 1, sym_first[0]).wait_send()
            for chunk in sym_first[1:]:
                sideways("j1", s1, 1, chunk).start()
            sideways("a1", a1, 1, 0, cross_peer).start()

        pass_sym("s1", s1, 1)

        @pl.when(half == 0)
        def _():
            for chunk in sym_first[1:]:
                sideways("j1", s1, 1, chunk).wait_recv()
                start_beside("s1", s1, 1, (chunk,))
            start_across("a1", a1, 0, all_chunks[1:])

        @pl.when(half == 1)
        def _():
            for chunk in all_chunks[1:]:
                sideways("j1", s1, 1, sym_first[1]).wait_send()
                sideways("a1", a1, 1, chunk, cross_peer).start()
            for chunk in all_chunks:
                sideways("a1", a1, 0, chunk).wait_recv()
                start_across("a1", a1, 0, (chunk,))

        gather_sym("s1", s1, 1)
        for kind, at, tag in ((0, core_peer, "c"), (1, side_peer, "x"), (0, cross_peer, "d")):
            vec1(kind, at, tag).wait_recv()

        @pl.when(half == 0)
        def _():
            for chunk in all_chunks:
                sideways("j1", s1, 2, chunk).start()

        def late_info():
            @pl.when(half == 1)
            def _():
                for chunk in all_chunks:
                    sideways("j1", s1, 2, chunk).wait_recv()

        def put_info(cols, value):
            j_out[:, cols] = value

        def send_info():
            copy("jo", j_out, j_out, core_peer).start()

        fresh = early_part(
            "a1", s1.at[0], s1.at[1], a1, v1, lambda cols: s1[2, :, wide(cols)],
            late_info, put_info, send_info, into(a_out),
        )
        copy("ao", a_out, a_out, core_peer).start()
        vec_out[1] = fresh
        copy("eo", vec_out.at[1], vec_out.at[1], core_peer).start()
        copy("co", c_out, c_out, core_peer).wait_recv()
        copy("bo", vec_out.at[0], vec_out.at[0], core_peer).wait_recv()
        for step in steps:
            for chunk in all_chunks:
                across("a0", a0, 0, step, chunk).wait_send()
                across("a1", a1, 0, step, chunk).wait_send()
        end_sends("s1", s1, 1)

        @pl.when(half == 0)
        def _():
            for chunk in all_chunks:
                sideways("j1", s1, 2, chunk).wait_send()
                sideways("a1", a1, 0, chunk).wait_send()

        @pl.when(half == 1)
        def _():
            for chunk in all_chunks:
                sideways("a1", a1, 1, chunk, cross_peer).wait_send()
                beside("a1", a1, 1, chunk).wait_send()

        for at, tag in vec1_peers:
            vec1(1, at, tag).wait_send()
        copy("jo", j_out, j_out, core_peer).wait_send()
        copy("ao", a_out, a_out, core_peer).wait_send()
        copy("eo", vec_out.at[1], vec_out.at[1], core_peer).wait_send()

    @pl.when(core == 1)
    def _():
        def store_cov(cols, value):
            s1[cov_slot, :, wide(cols)] = value

        fresh = late_part(
            "a0", s0.at[0], s0.at[1], a0, v0, lambda cols: c_ref[:, cols],
            lambda: None, store_cov
        )

        @pl.when(half == 0)
        def _():
            start_across("s1", s1, 0, sym_chunks)
            for chunk in sym_first:
                sideways("c1", s1, 0, chunk).start()
            start_beside("s1", s1, 0)

        share_vec(0, fresh)

        @pl.when(half == 1)
        def _():
            for chunk in all_chunks:
                beside("a1", a1, 1, chunk).wait_recv()
            start_across("a1", a1, 1, all_chunks[:1])
            sideways("c1", s1, 0, sym_first[0]).wait_recv()
            start_across("s1", s1, 0, sym_chunks)
            start_beside("s1", s1, 0, sym_first[:1])

        pass_sym("s1", s1, 0)

        @pl.when(half == 1)
        def _():
            for chunk in sym_first[1:]:
                sideways("c1", s1, 0, chunk).wait_recv()
                start_beside("s1", s1, 0, (chunk,))
            start_across("a1", a1, 1, all_chunks[1:])
            for chunk in all_chunks:
                sideways("c1", s1, 3, chunk).start()

        gather_sym("s1", s1, 0)
        for kind, at, tag in ((1, core_peer, "c"), (0, side_peer, "x"), (1, cross_peer, "d")):
            vec1(kind, at, tag).wait_recv()

        def late_cov():
            @pl.when(half == 0)
            def _():
                for chunk in all_chunks:
                    sideways("c1", s1, 3, chunk).wait_recv()

        def put_cov(cols, value):
            c_out[:, cols] = value

        fresh = late_part(
            "a1", s1.at[0], s1.at[1], a1, v1, lambda cols: s1[3, :, wide(cols)],
            late_cov, put_cov
        )
        copy("co", c_out, c_out, core_peer).start()
        vec_out[0] = fresh
        copy("bo", vec_out.at[0], vec_out.at[0], core_peer).start()
        copy("jo", j_out, j_out, core_peer).wait_recv()
        copy("ao", a_out, a_out, core_peer).wait_recv()
        copy("eo", vec_out.at[1], vec_out.at[1], core_peer).wait_recv()
        for step in steps:
            for chunk in all_chunks:
                for name, ref in (("a0", a0), ("a1", a1)):
                    across(name, ref, 1, step, chunk).wait_send()
                    onward(name, ref, 1, step, chunk).wait_send()
        for chunk in all_chunks:
            beside("a0", a0, 1, chunk).wait_send()
            sideways("c1", s1, cov_slot, chunk).wait_send()

        @pl.when(half == 0)
        def _():
            for chunk in all_chunks:
                beside("b1", a1, 1, chunk).wait_send()

        end_sends("s1", s1, 0)
        for at, tag in vec1_peers:
            vec1(0, at, tag).wait_send()
        copy("co", c_out, c_out, core_peer).wait_send()
        copy("bo", vec_out.at[0], vec_out.at[0], core_peer).wait_send()

    end_sends("s0", s0, core)
    vec0().wait_send()


def place(a_ref, c_ref, j_ref, vec_ref, a_out, b_out, c_out, eta_out, j_out, sems):
    moves = [
        pltpu.make_async_copy(src, dst, sems.at[index])
        for index, (src, dst) in enumerate(((a_ref, a_out), (c_ref, c_out), (j_ref, j_out)))
    ]
    for move in moves:
        move.start()
    b_out[...] = vec_ref[0, 0:1].astype(BF16)
    eta_out[...] = vec_ref[1, 0:1].astype(BF16)
    for move in moves:
        move.wait()


def local(panels, transition, drift, spread, belief, precision, probe_hosts, probe_values):
    states, width = transition.shape[1:]
    panel = jax.ShapeDtypeStruct((states, width), BF16)
    vmem = pl.BlockSpec(memory_space=pltpu.VMEM)
    square = (states, states)
    count = 48 + 16 * (panels - 1)
    combine = 2 * states * states * width
    a, c, j, vecs = pl.pallas_call(
        functools.partial(kernel, panels, {}),
        out_shape=(panel, panel, panel, jax.ShapeDtypeStruct((2, 16, states), F32)),
        in_specs=[vmem] * 7,
        out_specs=(vmem,) * 4,
        scratch_shapes=[
            pltpu.VMEM((2,) + square, BF16),
            pltpu.VMEM((2,) + square, BF16),
            pltpu.VMEM((4,) + square, BF16),
            pltpu.VMEM((2,) + square, BF16),
            pltpu.VMEM((2, 2, 16, states), F32),
            pltpu.VMEM((2, 2, 16, states), F32),
            pltpu.VMEM((states, width), BF16),
            pltpu.VMEM((states, width), BF16),
            pltpu.VMEM((states, width), BF16),
            pltpu.VMEM((states, width), BF16),
            pltpu.SemaphoreType.DMA((count,)),
            pltpu.SemaphoreType.DMA((count,)),
        ],
        compiler_params=pltpu.CompilerParams(
            collective_id=0, has_side_effects=True, vmem_limit_bytes=56 * 2**20
        ),
        cost_estimate=pl.CostEstimate(
            flops=18 * combine, bytes_accessed=12 * states * width, transcendentals=0
        ),
    )(
        transition[0], spread[0], precision[0], drift, belief, probe_hosts, probe_values
    )
    anywhere = pl.BlockSpec(memory_space=pl.ANY)
    row = jax.ShapeDtypeStruct((1, states), BF16)
    a, b, c, eta, j = pl.pallas_call(
        place,
        out_shape=(panel, row, panel, row, panel),
        in_specs=[anywhere] * 3 + [vmem],
        out_specs=(anywhere, vmem, anywhere, vmem, anywhere),
        scratch_shapes=[pltpu.SemaphoreType.DMA((3,))],
        cost_estimate=pl.CostEstimate(
            flops=0, bytes_accessed=12 * states * width, transcendentals=0
        ),
    )(a, c, j, vecs)
    return a[None], b, c[None], eta, j[None]


def solution(mesh):
    matrix = P("tm", None, "panel")
    vector = P("tm", None)
    return jax.shard_map(
        functools.partial(local, mesh.shape["panel"]),
        mesh=mesh,
        in_specs=(matrix, vector, matrix, vector, matrix, vector, vector),
        out_specs=(matrix, vector, matrix, vector, matrix),
        check_vma=False,
    )
```

```python
import functools

import jax
import jax.numpy as jnp
from jax import lax
from jax.experimental import pallas as pl
from jax.experimental.pallas import tpu as pltpu
from jax.sharding import PartitionSpec as P

NS = 2
TERMS = 2**NS - 1
F32 = jnp.float32
BF16 = jnp.bfloat16
MESH = pl.DeviceIdType.MESH
NN = (((1,), (0,)), ((), ()))
NT = (((1,), (1,)), ((), ()))
TN = (((0,), (0,)), ((), ()))


def dot(lhs, rhs, dims=NN):
    return lax.dot_general(lhs, rhs, dims, preferred_element_type=F32)


def kernel(
    panels, names,
    a_ref, c_ref, j_ref, b_ref, eta_ref, hosts_ref, values_ref,
    a_out, c_out, j_out, vec_out,
    s0, a0, s1, a1, v0, v1, anchor, cur, inner, weighted, send_sem, recv_sem,
):
    states, width = a_ref.shape
    tile = min(width, 256)
    tiles = width // tile
    time = lax.axis_index("tm")
    me = lax.axis_index("panel")
    core = lax.rem(time, 2)
    half = lax.rem(lax.div(time, 2), 2)
    core_peer = time + 1 - 2 * core
    side_peer = time + 2 - 4 * half
    cross_peer = core_peer + 2 - 4 * half
    own_cols = pl.ds(pl.multiple_of(me * width, width), width)

    def sem(name):
        return names.setdefault(name, len(names))

    def copy(name, src, dst, at, panel=None):
        index = sem(name)
        return pltpu.make_async_remote_copy(
            src_ref=src, dst_ref=dst,
            send_sem=send_sem.at[index], recv_sem=recv_sem.at[index],
            device_id=(at, me if panel is None else panel), device_id_type=MESH,
        )

    def panel_block(ref, slot, rows, cols):
        return ref.at[slot, rows, cols]

    def chunk_rows(target, chunk):
        if panels != 2:
            return pl.ds(0, states)
        block = lax.rem(target + chunk, 2)
        return pl.ds(pl.multiple_of(block * width, width), width)

    def cols_of(panel):
        return pl.ds(pl.multiple_of(panel * width, width), width)

    def across(name, ref, slot, step, chunk):
        target = lax.rem(me + step, panels)
        block = panel_block(ref, slot, chunk_rows(target, chunk), own_cols)
        return copy(f"{name}y{step}.{chunk}", block, block, time, target)

    def onward(name, ref, slot, step, chunk):
        source = lax.rem(me - step + panels, panels)
        block = panel_block(ref, slot, chunk_rows(me, chunk), cols_of(source))
        return copy(f"{name}f{step}.{chunk}", block, block, core_peer)

    def beside(name, ref, slot, chunk):
        block = panel_block(ref, slot, chunk_rows(me + 1, chunk), own_cols)
        return copy(f"{name}c{chunk}", block, block, core_peer)

    def sideways(name, ref, slot, chunk, at=side_peer):
        block = panel_block(ref, slot, chunk_rows(me + 1, chunk), own_cols)
        return copy(f"{name}x{chunk}", block, block, at)

    steps = range(1, panels)
    sym_chunks = (1,) if panels == 2 else (0,)
    all_chunks = (0, 1) if panels == 2 else (0,)
    sym_first = all_chunks[::-1]

    def products(lhs, rhs, dims, put):
        for index in range(tiles):
            cols = pl.ds(index * tile, tile)
            put(cols, dot(lhs[...], rhs(cols), dims))

    def into(ref):
        def put(cols, value):
            ref[:, cols] = value.astype(BF16)
        return put

    def series(cov, info):
        cur[...] = anchor[...]

        @pl.loop(0, TERMS)
        def _(repeat):
            products(info, lambda cols: cur[:, cols], NN, into(inner))

            def put(cols, value):
                cur[:, cols] = (anchor[:, cols].astype(F32) - value).astype(BF16)

            products(cov, lambda cols: inner[:, cols], NN, put)

    def vec_series(start, first, second):
        def step(repeat, vector):
            middle = dot(vector.astype(BF16), first[...])
            return start - dot(middle.astype(BF16), second[...])

        return lax.fori_loop(0, TERMS, step, start)

    def mirror(ref, slot):
        if panels == 2:
            other = pl.ds(pl.multiple_of((1 - me) * width, width), width)
            ref[slot, own_cols, other] = ref[slot, other, own_cols].T

    def start_across(name, ref, slot, chunks):
        for step in steps:
            for chunk in chunks:
                across(name, ref, slot, step, chunk).start()

    def start_beside(name, ref, slot, chunks=sym_first):
        for chunk in chunks:
            beside(name, ref, slot, chunk).start()

    def pass_sym(name, ref, slot):
        for step in steps:
            for chunk in sym_chunks:
                across(name, ref, slot, step, chunk).wait_recv()
                onward(name, ref, slot, step, chunk).start()

    def gather_sym(name, ref, slot):
        for chunk in sym_first:
            beside(name, ref, slot, chunk).wait_recv()
        for step in steps:
            for chunk in sym_chunks:
                onward(name, ref, slot, step, chunk).wait_recv()
        mirror(ref, 0)
        mirror(ref, 1)

    def end_sends(name, ref, slot):
        for step in steps:
            for chunk in sym_chunks:
                if name != "s0":
                    across(name, ref, slot, step, chunk).wait_send()
                onward(name, ref, slot, step, chunk).wait_send()
        for chunk in sym_first:
            beside(name, ref, slot, chunk).wait_send()

    barrier = pltpu.get_barrier_semaphore()
    for at in (core_peer, side_peer, cross_peer):
        pl.semaphore_signal(barrier, inc=1, device_id=(at, me), device_id_type=MESH)
    for step in steps:
        pl.semaphore_signal(
            barrier, inc=1, device_id=(time, lax.rem(me + step, panels)), device_id_type=MESH
        )
    pl.semaphore_wait(barrier, 3 + len(steps))

    @pl.when(core == 0)
    def _():
        s0[0, :, own_cols] = c_ref[...]

    @pl.when(core == 1)
    def _():
        s0[1, :, own_cols] = j_ref[...]

    start_across("s0", s0, core, sym_chunks)
    start_beside("s0", s0, core)
    a0[core, :, own_cols] = a_ref[...]

    @pl.when(core == 1)
    def _():
        start_beside("a0", a0, 1, all_chunks)

    hosts = jnp.broadcast_to(hosts_ref[...].astype(F32) * 2.0, (8, hosts_ref.shape[1])).T[:, :1]
    values = jnp.broadcast_to(values_ref[...], (8, values_ref.shape[1])).T[:, :1]
    spots = lax.broadcasted_iota(jnp.int32, (hosts.shape[0], states), 1).astype(F32)
    paired = jnp.sum(jnp.where(hosts == spots, values, 0.0), axis=0, keepdims=True)
    belief = (eta_ref[...].astype(F32) + paired).astype(BF16).astype(F32)
    v0[core, 0] = jnp.broadcast_to(b_ref[...].astype(F32), (16, states))
    v0[core, 1] = jnp.broadcast_to(belief, (16, states))

    def vec0():
        return copy("v0", v0.at[core], v0.at[core], core_peer)

    vec0().start()
    for step in steps:
        for chunk in sym_chunks:
            across("s0", s0, core, step, chunk).wait_send()
    start_across("a0", a0, core, all_chunks)
    pass_sym("s0", s0, core)
    gather_sym("s0", s0, core)
    vec0().wait_recv()

    def vec1(kind, at, tag):
        block = v1.at[half, kind]
        return copy(f"v1{kind}{tag}", block, block, at)

    vec1_peers = ((core_peer, "c"), (side_peer, "x"), (cross_peer, "d"))

    def late_part(name, cov, info, moves, vecs, addend, ready, store):
        start = vecs[0, 0] + dot(vecs[1, 1].astype(BF16), cov[...])
        forward = vec_series(start, info, cov)
        if name == "a1":
            @pl.when(half == 0)
            def _():
                for chunk in all_chunks:
                    sideways("a1", a1, 1, chunk).wait_recv()
                    start_across("a1", a1, 1, (chunk,))
                    beside("b1", a1, 1, chunk).start()

        for step in steps:
            across(name, moves, 1, step, 0).wait_recv()
            onward(name, moves, 1, step, 0).start()
        own_rows = me * width

        def rows(cols):
            return moves[1, pl.ds(pl.multiple_of(own_rows + cols.start, tile), tile), :]

        products(cov, rows, NT, into(anchor))
        series(cov, info)
        for step in steps:
            for chunk in all_chunks[1:]:
                across(name, moves, 1, step, chunk).wait_recv()
                onward(name, moves, 1, step, chunk).start()

        ready()

        def put(cols, value):
            store(cols, (value + addend(cols).astype(F32)).astype(BF16))

        products(moves.at[1], lambda cols: cur[:, cols], NN, put)
        fresh = dot(forward.astype(BF16), moves[1], NT) + vecs[1, 0]
        return fresh.astype(BF16).astype(F32)

    def early_part(name, cov, info, moves, vecs, addend, ready_info, store_info, sent_info, store_move):
        anchor[...] = moves[0, :, own_cols]
        series(cov, info)
        products(info, lambda cols: cur[:, cols], NN, into(weighted))
        start = vecs[1, 1] - dot(vecs[0, 0].astype(BF16), info[...])
        backward = vec_series(start, cov, info)
        for step in steps:
            for chunk in all_chunks:
                across(name, moves, 0, step, chunk).wait_recv()

        ready_info()

        def put(cols, value):
            store_info(cols, (value + addend(cols).astype(F32)).astype(BF16))

        products(moves.at[0], lambda cols: weighted[:, cols], TN, put)
        sent_info()
        fresh = dot(backward.astype(BF16), moves[0]) + vecs[0, 1]
        if name == "a0":
            for chunk in all_chunks:
                beside(name, moves, 1, chunk).wait_recv()
        else:
            @pl.when(half == 0)
            def _():
                for chunk in all_chunks:
                    beside("b1", moves, 1, chunk).wait_recv()

        for step in steps:
            for chunk in all_chunks:
                onward(name, moves, 1, step, chunk).wait_recv()
        products(moves.at[1], lambda cols: cur[:, cols], NN, store_move)
        return fresh.astype(BF16).astype(F32)

    info_slot = 2 - half
    cov_slot = 3 * half

    def wide(cols):
        return pl.ds(pl.multiple_of(me * width + cols.start, tile), tile)

    def share_vec(kind, value):
        v1[half, kind] = value
        for at, tag in vec1_peers:
            vec1(kind, at, tag).start()

    @pl.when(core == 0)
    def _():
        def store_info(cols, value):
            s1[info_slot, :, wide(cols)] = value

        def store_move(cols, value):
            a1[half, :, wide(cols)] = value.astype(BF16)

        def sent_info():
            @pl.when(half == 1)
            def _():
                sideways("j1", s1, 1, sym_first[0]).start()
                start_across("s1", s1, 1, sym_chunks)
                start_beside("s1", s1, 1)

        fresh = early_part(
            "a0", s0.at[0], s0.at[1], a0, v0, lambda cols: j_ref[:, cols],
            lambda: None, store_info, sent_info, store_move,
        )
        share_vec(1, fresh)

        @pl.when(half == 0)
        def _():
            for chunk in all_chunks:
                sideways("a1", a1, 0, chunk).start()
            start_across("a1", a1, 0, all_chunks[:1])
            sideways("j1", s1, 1, sym_first[0]).wait_recv()
            start_across("s1", s1, 1, sym_chunks)
            start_beside("s1", s1, 1, sym_first[:1])

        @pl.when(half == 1)
        def _():
            start_beside("a1", a1, 1, all_chunks)
            sideways("j1", s1, 1, sym_first[0]).wait_send()
            for chunk in sym_first[1:]:
                sideways("j1", s1, 1, chunk).start()
            sideways("a1", a1, 1, 0, cross_peer).start()

        pass_sym("s1", s1, 1)

        @pl.when(half == 0)
        def _():
            for chunk in sym_first[1:]:
                sideways("j1", s1, 1, chunk).wait_recv()
                start_beside("s1", s1, 1, (chunk,))
            start_across("a1", a1, 0, all_chunks[1:])

        @pl.when(half == 1)
        def _():
            for chunk in all_chunks[1:]:
                sideways("j1", s1, 1, sym_first[1]).wait_send()
                sideways("a1", a1, 1, chunk, cross_peer).start()
            for chunk in all_chunks:
                sideways("a1", a1, 0, chunk).wait_recv()
                start_across("a1", a1, 0, (chunk,))

        gather_sym("s1", s1, 1)
        for kind, at, tag in ((0, core_peer, "c"), (1, side_peer, "x"), (0, cross_peer, "d")):
            vec1(kind, at, tag).wait_recv()

        @pl.when(half == 0)
        def _():
            for chunk in all_chunks:
                sideways("j1", s1, 2, chunk).start()

        def late_info():
            @pl.when(half == 1)
            def _():
                for chunk in all_chunks:
                    sideways("j1", s1, 2, chunk).wait_recv()

        def put_info(cols, value):
            j_out[:, cols] = value

        def send_info():
            copy("jo", j_out, j_out, core_peer).start()

        fresh = early_part(
            "a1", s1.at[0], s1.at[1], a1, v1, lambda cols: s1[2, :, wide(cols)],
            late_info, put_info, send_info, into(a_out),
        )
        copy("ao", a_out, a_out, core_peer).start()
        vec_out[1] = fresh
        copy("eo", vec_out.at[1], vec_out.at[1], core_peer).start()
        copy("co", c_out, c_out, core_peer).wait_recv()
        copy("bo", vec_out.at[0], vec_out.at[0], core_peer).wait_recv()
        for step in steps:
            for chunk in all_chunks:
                across("a0", a0, 0, step, chunk).wait_send()
                across("a1", a1, 0, step, chunk).wait_send()
        end_sends("s1", s1, 1)

        @pl.when(half == 0)
        def _():
            for chunk in all_chunks:
                sideways("j1", s1, 2, chunk).wait_send()
                sideways("a1", a1, 0, chunk).wait_send()

        @pl.when(half == 1)
        def _():
            for chunk in all_chunks:
                sideways("a1", a1, 1, chunk, cross_peer).wait_send()
                beside("a1", a1, 1, chunk).wait_send()

        for at, tag in vec1_peers:
            vec1(1, at, tag).wait_send()
        copy("jo", j_out, j_out, core_peer).wait_send()
        copy("ao", a_out, a_out, core_peer).wait_send()
        copy("eo", vec_out.at[1], vec_out.at[1], core_peer).wait_send()

    @pl.when(core == 1)
    def _():
        def store_cov(cols, value):
            s1[cov_slot, :, wide(cols)] = value

        fresh = late_part(
            "a0", s0.at[0], s0.at[1], a0, v0, lambda cols: c_ref[:, cols],
            lambda: None, store_cov
        )

        @pl.when(half == 0)
        def _():
            start_across("s1", s1, 0, sym_chunks)
            for chunk in sym_first:
                sideways("c1", s1, 0, chunk).start()
            start_beside("s1", s1, 0)

        share_vec(0, fresh)

        @pl.when(half == 1)
        def _():
            for chunk in all_chunks:
                beside("a1", a1, 1, chunk).wait_recv()
            start_across("a1", a1, 1, all_chunks[:1])
            sideways("c1", s1, 0, sym_first[0]).wait_recv()
            start_across("s1", s1, 0, sym_chunks)
            start_beside("s1", s1, 0, sym_first[:1])

        pass_sym("s1", s1, 0)

        @pl.when(half == 1)
        def _():
            for chunk in sym_first[1:]:
                sideways("c1", s1, 0, chunk).wait_recv()
                start_beside("s1", s1, 0, (chunk,))
            start_across("a1", a1, 1, all_chunks[1:])
            for chunk in all_chunks:
                sideways("c1", s1, 3, chunk).start()

        gather_sym("s1", s1, 0)
        for kind, at, tag in ((1, core_peer, "c"), (0, side_peer, "x"), (1, cross_peer, "d")):
            vec1(kind, at, tag).wait_recv()

        def late_cov():
            @pl.when(half == 0)
            def _():
                for chunk in all_chunks:
                    sideways("c1", s1, 3, chunk).wait_recv()

        def put_cov(cols, value):
            c_out[:, cols] = value

        fresh = late_part(
            "a1", s1.at[0], s1.at[1], a1, v1, lambda cols: s1[3, :, wide(cols)],
            late_cov, put_cov
        )
        copy("co", c_out, c_out, core_peer).start()
        vec_out[0] = fresh
        copy("bo", vec_out.at[0], vec_out.at[0], core_peer).start()
        copy("jo", j_out, j_out, core_peer).wait_recv()
        copy("ao", a_out, a_out, core_peer).wait_recv()
        copy("eo", vec_out.at[1], vec_out.at[1], core_peer).wait_recv()
        for step in steps:
            for chunk in all_chunks:
                for name, ref in (("a0", a0), ("a1", a1)):
                    across(name, ref, 1, step, chunk).wait_send()
                    onward(name, ref, 1, step, chunk).wait_send()
        for chunk in all_chunks:
            beside("a0", a0, 1, chunk).wait_send()
            sideways("c1", s1, cov_slot, chunk).wait_send()

        @pl.when(half == 0)
        def _():
            for chunk in all_chunks:
                beside("b1", a1, 1, chunk).wait_send()

        end_sends("s1", s1, 0)
        for at, tag in vec1_peers:
            vec1(0, at, tag).wait_send()
        copy("co", c_out, c_out, core_peer).wait_send()
        copy("bo", vec_out.at[0], vec_out.at[0], core_peer).wait_send()

    end_sends("s0", s0, core)
    vec0().wait_send()


def place(a_ref, c_ref, j_ref, vec_ref, a_out, b_out, c_out, eta_out, j_out, held, sems):
    pieces = held.shape[1]
    rows = held.shape[2]
    fetches, sends = [], []
    for index, (src, dst) in enumerate(((a_ref, a_out), (c_ref, c_out), (j_ref, j_out))):
        for piece in range(pieces):
            block = pl.ds(piece * rows, rows)
            slot = held.at[index, piece]
            fetches.append(pltpu.make_async_copy(src.at[block], slot, sems.at[0, index, piece]))
            sends.append(pltpu.make_async_copy(slot, dst.at[block], sems.at[1, index, piece]))
    for fetch in fetches:
        fetch.start()
    b_out[...] = vec_ref[0, 0:1].astype(BF16)
    eta_out[...] = vec_ref[1, 0:1].astype(BF16)
    for fetch, send in zip(fetches, sends):
        fetch.wait()
        send.start()
    for send in sends:
        send.wait()


def local(panels, transition, drift, spread, belief, precision, probe_hosts, probe_values):
    states, width = transition.shape[1:]
    panel = jax.ShapeDtypeStruct((states, width), BF16)
    vmem = pl.BlockSpec(memory_space=pltpu.VMEM)
    square = (states, states)
    count = 48 + 16 * (panels - 1)
    combine = 2 * states * states * width
    a, c, j, vecs = pl.pallas_call(
        functools.partial(kernel, panels, {}),
        out_shape=(panel, panel, panel, jax.ShapeDtypeStruct((2, 16, states), F32)),
        in_specs=[vmem] * 7,
        out_specs=(vmem,) * 4,
        scratch_shapes=[
            pltpu.VMEM((2,) + square, BF16),
            pltpu.VMEM((2,) + square, BF16),
            pltpu.VMEM((4,) + square, BF16),
            pltpu.VMEM((2,) + square, BF16),
            pltpu.VMEM((2, 2, 16, states), F32),
            pltpu.VMEM((2, 2, 16, states), F32),
            pltpu.VMEM((states, width), BF16),
            pltpu.VMEM((states, width), BF16),
            pltpu.VMEM((states, width), BF16),
            pltpu.VMEM((states, width), BF16),
            pltpu.SemaphoreType.DMA((count,)),
            pltpu.SemaphoreType.DMA((count,)),
        ],
        compiler_params=pltpu.CompilerParams(
            collective_id=0, has_side_effects=True, vmem_limit_bytes=56 * 2**20
        ),
        cost_estimate=pl.CostEstimate(
            flops=18 * combine, bytes_accessed=12 * states * width, transcendentals=0
        ),
    )(
        transition[0], spread[0], precision[0], drift, belief, probe_hosts, probe_values
    )
    anywhere = pl.BlockSpec(memory_space=pl.ANY)
    row = jax.ShapeDtypeStruct((1, states), BF16)
    a, b, c, eta, j = pl.pallas_call(
        place,
        out_shape=(panel, row, panel, row, panel),
        in_specs=[anywhere] * 3 + [vmem],
        out_specs=(anywhere, vmem, anywhere, vmem, anywhere),
        scratch_shapes=[
            pltpu.VMEM((3, 2, states // 2, width), BF16),
            pltpu.SemaphoreType.DMA((2, 3, 2)),
        ],
        cost_estimate=pl.CostEstimate(
            flops=0, bytes_accessed=12 * states * width, transcendentals=0
        ),
    )(a, c, j, vecs)
    return a[None], b, c[None], eta, j[None]


def solution(mesh):
    matrix = P("tm", None, "panel")
    vector = P("tm", None)
    return jax.shard_map(
        functools.partial(local, mesh.shape["panel"]),
        mesh=mesh,
        in_specs=(matrix, vector, matrix, vector, matrix, vector, vector),
        out_specs=(matrix, vector, matrix, vector, matrix),
        check_vma=False,
    )
```

```python
import functools

import jax
import jax.numpy as jnp
from jax import lax
from jax.experimental import pallas as pl
from jax.experimental.pallas import tpu as pltpu
from jax.sharding import PartitionSpec as P

NS = 2
TERMS = 2**NS - 1
F32 = jnp.float32
BF16 = jnp.bfloat16
MESH = pl.DeviceIdType.MESH
NN = (((1,), (0,)), ((), ()))
NT = (((1,), (1,)), ((), ()))
TN = (((0,), (0,)), ((), ()))


def dot(lhs, rhs, dims=NN):
    return lax.dot_general(lhs, rhs, dims, preferred_element_type=F32)


def kernel(
    panels, names,
    a_ref, c_ref, j_ref, b_ref, eta_ref, hosts_ref, values_ref,
    a_out, c_out, j_out, vec_out,
    s0, a0, s1, a1, v0, v1, anchor, cur, inner, weighted, send_sem, recv_sem, place_sem,
):
    states, width = a_ref.shape
    tile = min(width, 256)
    tiles = width // tile
    time = lax.axis_index("tm")
    me = lax.axis_index("panel")
    core = lax.rem(time, 2)
    half = lax.rem(lax.div(time, 2), 2)
    core_peer = time + 1 - 2 * core
    side_peer = time + 2 - 4 * half
    cross_peer = core_peer + 2 - 4 * half
    own_cols = pl.ds(pl.multiple_of(me * width, width), width)

    def sem(name):
        return names.setdefault(name, len(names))

    def copy(name, src, dst, at, panel=None):
        index = sem(name)
        return pltpu.make_async_remote_copy(
            src_ref=src, dst_ref=dst,
            send_sem=send_sem.at[index], recv_sem=recv_sem.at[index],
            device_id=(at, me if panel is None else panel), device_id_type=MESH,
        )

    def panel_block(ref, slot, rows, cols):
        return ref.at[slot, rows, cols]

    def chunk_rows(target, chunk):
        if panels != 2:
            return pl.ds(0, states)
        block = lax.rem(target + chunk, 2)
        return pl.ds(pl.multiple_of(block * width, width), width)

    def cols_of(panel):
        return pl.ds(pl.multiple_of(panel * width, width), width)

    def across(name, ref, slot, step, chunk):
        target = lax.rem(me + step, panels)
        block = panel_block(ref, slot, chunk_rows(target, chunk), own_cols)
        return copy(f"{name}y{step}.{chunk}", block, block, time, target)

    def onward(name, ref, slot, step, chunk):
        source = lax.rem(me - step + panels, panels)
        block = panel_block(ref, slot, chunk_rows(me, chunk), cols_of(source))
        return copy(f"{name}f{step}.{chunk}", block, block, core_peer)

    def beside(name, ref, slot, chunk):
        block = panel_block(ref, slot, chunk_rows(me + 1, chunk), own_cols)
        return copy(f"{name}c{chunk}", block, block, core_peer)

    def sideways(name, ref, slot, chunk, at=side_peer):
        block = panel_block(ref, slot, chunk_rows(me + 1, chunk), own_cols)
        return copy(f"{name}x{chunk}", block, block, at)

    steps = range(1, panels)
    sym_chunks = (1,) if panels == 2 else (0,)
    all_chunks = (0, 1) if panels == 2 else (0,)
    sym_first = all_chunks[::-1]

    def products(lhs, rhs, dims, put):
        for index in range(tiles):
            cols = pl.ds(index * tile, tile)
            put(cols, dot(lhs[...], rhs(cols), dims))

    def into(ref):
        def put(cols, value):
            ref[:, cols] = value.astype(BF16)
        return put

    def series(cov, info):
        cur[...] = anchor[...]

        @pl.loop(0, TERMS)
        def _(repeat):
            products(info, lambda cols: cur[:, cols], NN, into(inner))

            def put(cols, value):
                cur[:, cols] = (anchor[:, cols].astype(F32) - value).astype(BF16)

            products(cov, lambda cols: inner[:, cols], NN, put)

    def vec_series(start, first, second):
        def step(repeat, vector):
            middle = dot(vector.astype(BF16), first[...])
            return start - dot(middle.astype(BF16), second[...])

        return lax.fori_loop(0, TERMS, step, start)

    def mirror(ref, slot):
        if panels == 2:
            other = pl.ds(pl.multiple_of((1 - me) * width, width), width)
            ref[slot, own_cols, other] = ref[slot, other, own_cols].T

    def start_across(name, ref, slot, chunks):
        for step in steps:
            for chunk in chunks:
                across(name, ref, slot, step, chunk).start()

    def start_beside(name, ref, slot, chunks=sym_first):
        for chunk in chunks:
            beside(name, ref, slot, chunk).start()

    def pass_sym(name, ref, slot):
        for step in steps:
            for chunk in sym_chunks:
                across(name, ref, slot, step, chunk).wait_recv()
                onward(name, ref, slot, step, chunk).start()

    def gather_sym(name, ref, slot):
        for chunk in sym_first:
            beside(name, ref, slot, chunk).wait_recv()
        for step in steps:
            for chunk in sym_chunks:
                onward(name, ref, slot, step, chunk).wait_recv()
        mirror(ref, 0)
        mirror(ref, 1)

    def end_sends(name, ref, slot):
        for step in steps:
            for chunk in sym_chunks:
                if name != "s0":
                    across(name, ref, slot, step, chunk).wait_send()
                onward(name, ref, slot, step, chunk).wait_send()
        for chunk in sym_first:
            beside(name, ref, slot, chunk).wait_send()

    def keep(name, src, dst, index):
        cols = pl.ds(index * tile, tile)
        return pltpu.make_async_copy(
            src.at[:, cols], dst.at[:, cols], place_sem.at[sem(f"{name}{index}")]
        )

    def share(name, src, dst, index):
        cols = pl.ds(index * tile, tile)
        return copy(f"{name}{index}", src.at[:, cols], dst.at[:, cols], core_peer)

    def start_result(name, src, dst, cols):
        share(name, src, dst, cols.start // tile).start()
        keep(name, src, dst, cols.start // tile).start()

    def end_results(name, src, dst):
        for index in range(tiles):
            keep(name, src, dst, index).wait()
            share(name, src, dst, index).wait_send()

    def end_arrivals(name, src, dst):
        for index in range(tiles):
            share(name, src, dst, index).wait_recv()

    barrier = pltpu.get_barrier_semaphore()
    for at in (core_peer, side_peer, cross_peer):
        pl.semaphore_signal(barrier, inc=1, device_id=(at, me), device_id_type=MESH)
    for step in steps:
        pl.semaphore_signal(
            barrier, inc=1, device_id=(time, lax.rem(me + step, panels)), device_id_type=MESH
        )
    pl.semaphore_wait(barrier, 3 + len(steps))

    @pl.when(core == 0)
    def _():
        s0[0, :, own_cols] = c_ref[...]

    @pl.when(core == 1)
    def _():
        s0[1, :, own_cols] = j_ref[...]

    start_across("s0", s0, core, sym_chunks)
    start_beside("s0", s0, core)
    a0[core, :, own_cols] = a_ref[...]

    @pl.when(core == 1)
    def _():
        start_beside("a0", a0, 1, all_chunks)

    hosts = jnp.broadcast_to(hosts_ref[...].astype(F32) * 2.0, (8, hosts_ref.shape[1])).T[:, :1]
    values = jnp.broadcast_to(values_ref[...], (8, values_ref.shape[1])).T[:, :1]
    spots = lax.broadcasted_iota(jnp.int32, (hosts.shape[0], states), 1).astype(F32)
    paired = jnp.sum(jnp.where(hosts == spots, values, 0.0), axis=0, keepdims=True)
    belief = (eta_ref[...].astype(F32) + paired).astype(BF16).astype(F32)
    v0[core, 0] = jnp.broadcast_to(b_ref[...].astype(F32), (16, states))
    v0[core, 1] = jnp.broadcast_to(belief, (16, states))

    def vec0():
        return copy("v0", v0.at[core], v0.at[core], core_peer)

    vec0().start()
    for step in steps:
        for chunk in sym_chunks:
            across("s0", s0, core, step, chunk).wait_send()
    start_across("a0", a0, core, all_chunks[:1])
    pass_sym("s0", s0, core)
    gather_sym("s0", s0, core)
    vec0().wait_recv()

    def vec1(kind, at, tag):
        block = v1.at[half, kind]
        return copy(f"v1{kind}{tag}", block, block, at)

    vec1_peers = ((core_peer, "c"), (side_peer, "x"), (cross_peer, "d"))

    def take_move(chunks):
        for chunk in chunks:
            sideways("a1", a1, 1, chunk).wait_recv()
            start_across("a1", a1, 1, (chunk,))
            beside("b1", a1, 1, chunk).start()

    def late_part(name, cov, info, moves, vecs, addend, ready, store):
        start = vecs[0, 0] + dot(vecs[1, 1].astype(BF16), cov[...])
        forward = vec_series(start, info, cov)
        if name == "a1":
            @pl.when(half == 0)
            def _():
                take_move(all_chunks[1:])

        for step in steps:
            across(name, moves, 1, step, 0).wait_recv()
        if name == "a0":
            start_across("a0", a0, 1, all_chunks[1:])
        for step in steps:
            onward(name, moves, 1, step, 0).start()
        own_rows = me * width

        def rows(cols):
            return moves[1, pl.ds(pl.multiple_of(own_rows + cols.start, tile), tile), :]

        products(cov, rows, NT, into(anchor))
        series(cov, info)
        for step in steps:
            for chunk in all_chunks[1:]:
                across(name, moves, 1, step, chunk).wait_recv()
                onward(name, moves, 1, step, chunk).start()

        ready()

        def put(cols, value):
            store(cols, (value + addend(cols).astype(F32)).astype(BF16))

        products(moves.at[1], lambda cols: cur[:, cols], NN, put)
        fresh = dot(forward.astype(BF16), moves[1], NT) + vecs[1, 0]
        return fresh.astype(BF16).astype(F32)

    def early_part(name, cov, info, moves, vecs, addend, ready_info, store_info, sent_info, store_move):
        def vector():
            start = vecs[1, 1] - dot(vecs[0, 0].astype(BF16), info[...])
            return vec_series(start, cov, info)

        if name == "a1":
            backward = vector()

            @pl.when(half == 1)
            def _():
                for chunk in all_chunks:
                    sideways("a1", a1, 0, chunk).wait_recv()
                    start_across("a1", a1, 0, (chunk,))

        anchor[...] = moves[0, :, own_cols]
        series(cov, info)
        if name == "a0":
            start_across("a0", a0, 0, all_chunks[1:])
        products(info, lambda cols: cur[:, cols], NN, into(weighted))
        if name == "a0":
            backward = vector()
        for step in steps:
            for chunk in all_chunks:
                across(name, moves, 0, step, chunk).wait_recv()

        ready_info()

        def put(cols, value):
            store_info(cols, (value + addend(cols).astype(F32)).astype(BF16))

        products(moves.at[0], lambda cols: weighted[:, cols], TN, put)
        sent_info()
        fresh = dot(backward.astype(BF16), moves[0]) + vecs[0, 1]
        if name == "a0":
            for chunk in all_chunks:
                beside(name, moves, 1, chunk).wait_recv()
        else:
            @pl.when(half == 0)
            def _():
                for chunk in all_chunks:
                    beside("b1", moves, 1, chunk).wait_recv()

        for step in steps:
            for chunk in all_chunks:
                onward(name, moves, 1, step, chunk).wait_recv()
        products(moves.at[1], lambda cols: cur[:, cols], NN, store_move)
        return fresh.astype(BF16).astype(F32)

    info_slot = 2 - half
    cov_slot = 3 * half

    def wide(cols):
        return pl.ds(pl.multiple_of(me * width + cols.start, tile), tile)

    def share_vec(kind, value):
        v1[half, kind] = value
        for at, tag in vec1_peers:
            vec1(kind, at, tag).start()

    @pl.when(core == 0)
    def _():
        def store_info(cols, value):
            s1[info_slot, :, wide(cols)] = value

        def store_move(cols, value):
            a1[half, :, wide(cols)] = value.astype(BF16)

        def sent_info():
            @pl.when(half == 1)
            def _():
                sideways("j1", s1, 1, sym_first[0]).start()
                start_across("s1", s1, 1, sym_chunks)
                start_beside("s1", s1, 1)

        fresh = early_part(
            "a0", s0.at[0], s0.at[1], a0, v0, lambda cols: j_ref[:, cols],
            lambda: None, store_info, sent_info, store_move,
        )
        share_vec(1, fresh)

        @pl.when(half == 0)
        def _():
            sideways("j1", s1, 1, sym_first[0]).wait_recv()
            start_across("s1", s1, 1, sym_chunks)
            start_beside("s1", s1, 1, sym_first[:1])
            sideways("a1", a1, 0, 0).start()

        @pl.when(half == 1)
        def _():
            start_beside("a1", a1, 1, all_chunks)
            sideways("j1", s1, 1, sym_first[0]).wait_send()
            sideways("a1", a1, 1, 0, cross_peer).start()

        pass_sym("s1", s1, 1)

        @pl.when(half == 0)
        def _():
            for chunk in all_chunks[1:]:
                sideways("a1", a1, 0, chunk).start()
            for chunk in sym_first[1:]:
                sideways("j1", s1, 1, chunk).wait_recv()
                start_beside("s1", s1, 1, (chunk,))
            start_across("a1", a1, 0, all_chunks)

        @pl.when(half == 1)
        def _():
            sideways("a1", a1, 1, 0, cross_peer).wait_send()
            for chunk in sym_first[1:]:
                sideways("j1", s1, 1, chunk).start()
                sideways("j1", s1, 1, chunk).wait_send()
            for chunk in all_chunks[1:]:
                sideways("a1", a1, 1, chunk, cross_peer).start()

        gather_sym("s1", s1, 1)
        for kind, at, tag in ((0, core_peer, "c"), (1, side_peer, "x"), (0, cross_peer, "d")):
            vec1(kind, at, tag).wait_recv()

        @pl.when(half == 0)
        def _():
            for chunk in all_chunks:
                sideways("j1", s1, 2, chunk).start()

        def late_info():
            @pl.when(half == 1)
            def _():
                for chunk in all_chunks:
                    sideways("j1", s1, 2, chunk).wait_recv()

        def put_info(cols, value):
            inner[:, cols] = value
            start_result("jo", inner, j_out, cols)

        def put_move(cols, value):
            anchor[:, cols] = value.astype(BF16)
            start_result("ao", anchor, a_out, cols)

        fresh = early_part(
            "a1", s1.at[0], s1.at[1], a1, v1, lambda cols: s1[2, :, wide(cols)],
            late_info, put_info, lambda: None, put_move,
        )
        vec_out[1] = fresh
        copy("eo", vec_out.at[1], vec_out.at[1], core_peer).start()
        end_arrivals("co", weighted, c_out)
        copy("bo", vec_out.at[0], vec_out.at[0], core_peer).wait_recv()
        for step in steps:
            for chunk in all_chunks:
                across("a0", a0, 0, step, chunk).wait_send()
                across("a1", a1, 0, step, chunk).wait_send()
        end_sends("s1", s1, 1)

        @pl.when(half == 0)
        def _():
            for chunk in all_chunks:
                sideways("j1", s1, 2, chunk).wait_send()
                sideways("a1", a1, 0, chunk).wait_send()

        @pl.when(half == 1)
        def _():
            for chunk in all_chunks[1:]:
                sideways("a1", a1, 1, chunk, cross_peer).wait_send()
            for chunk in all_chunks:
                beside("a1", a1, 1, chunk).wait_send()

        for at, tag in vec1_peers:
            vec1(1, at, tag).wait_send()
        end_results("jo", inner, j_out)
        end_results("ao", anchor, a_out)
        copy("eo", vec_out.at[1], vec_out.at[1], core_peer).wait_send()

    @pl.when(core == 1)
    def _():
        def store_cov(cols, value):
            s1[cov_slot, :, wide(cols)] = value

        fresh = late_part(
            "a0", s0.at[0], s0.at[1], a0, v0, lambda cols: c_ref[:, cols],
            lambda: None, store_cov
        )

        @pl.when(half == 0)
        def _():
            start_across("s1", s1, 0, sym_chunks)
            for chunk in sym_first:
                sideways("c1", s1, 0, chunk).start()
            start_beside("s1", s1, 0)

        share_vec(0, fresh)

        @pl.when(half == 1)
        def _():
            for chunk in all_chunks:
                beside("a1", a1, 1, chunk).wait_recv()
            start_across("a1", a1, 1, all_chunks[:1])
            sideways("c1", s1, 0, sym_first[0]).wait_recv()
            start_across("s1", s1, 0, sym_chunks)
            start_beside("s1", s1, 0, sym_first[:1])

        pass_sym("s1", s1, 0)

        @pl.when(half == 1)
        def _():
            for chunk in sym_first[1:]:
                sideways("c1", s1, 0, chunk).wait_recv()
                start_beside("s1", s1, 0, (chunk,))
            start_across("a1", a1, 1, all_chunks[1:])
            for chunk in all_chunks:
                sideways("c1", s1, 3, chunk).start()

        @pl.when(half == 0)
        def _():
            take_move(all_chunks[:1])

        gather_sym("s1", s1, 0)
        for kind, at, tag in ((1, core_peer, "c"), (0, side_peer, "x"), (1, cross_peer, "d")):
            vec1(kind, at, tag).wait_recv()

        def late_cov():
            @pl.when(half == 0)
            def _():
                for chunk in all_chunks:
                    sideways("c1", s1, 3, chunk).wait_recv()

        def put_cov(cols, value):
            weighted[:, cols] = value
            start_result("co", weighted, c_out, cols)

        fresh = late_part(
            "a1", s1.at[0], s1.at[1], a1, v1, lambda cols: s1[3, :, wide(cols)],
            late_cov, put_cov
        )
        vec_out[0] = fresh
        copy("bo", vec_out.at[0], vec_out.at[0], core_peer).start()
        end_arrivals("jo", inner, j_out)
        end_arrivals("ao", anchor, a_out)
        copy("eo", vec_out.at[1], vec_out.at[1], core_peer).wait_recv()
        for step in steps:
            for chunk in all_chunks:
                for name, ref in (("a0", a0), ("a1", a1)):
                    across(name, ref, 1, step, chunk).wait_send()
                    onward(name, ref, 1, step, chunk).wait_send()
        for chunk in all_chunks:
            beside("a0", a0, 1, chunk).wait_send()
            sideways("c1", s1, cov_slot, chunk).wait_send()

        @pl.when(half == 0)
        def _():
            for chunk in all_chunks:
                beside("b1", a1, 1, chunk).wait_send()

        end_sends("s1", s1, 0)
        for at, tag in vec1_peers:
            vec1(0, at, tag).wait_send()
        end_results("co", weighted, c_out)
        copy("bo", vec_out.at[0], vec_out.at[0], core_peer).wait_send()

    end_sends("s0", s0, core)
    vec0().wait_send()


def place(a_ref, c_ref, j_ref, vec_ref, a_out, b_out, c_out, eta_out, j_out, held, sems):
    pieces = held.shape[1]
    rows = held.shape[2]
    fetches, sends = [], []
    for index, (src, dst) in enumerate(((a_ref, a_out), (c_ref, c_out), (j_ref, j_out))):
        for piece in range(pieces):
            block = pl.ds(piece * rows, rows)
            slot = held.at[index, piece]
            fetches.append(pltpu.make_async_copy(src.at[block], slot, sems.at[0, index, piece]))
            sends.append(pltpu.make_async_copy(slot, dst.at[block], sems.at[1, index, piece]))
    for fetch in fetches:
        fetch.start()
    b_out[...] = vec_ref[0, 0:1].astype(BF16)
    eta_out[...] = vec_ref[1, 0:1].astype(BF16)
    for fetch, send in zip(fetches, sends):
        fetch.wait()
        send.start()
    for send in sends:
        send.wait()


def local(panels, transition, drift, spread, belief, precision, probe_hosts, probe_values):
    states, width = transition.shape[1:]
    panel = jax.ShapeDtypeStruct((states, width), BF16)
    vmem = pl.BlockSpec(memory_space=pltpu.VMEM)
    anywhere = pl.BlockSpec(memory_space=pl.ANY)
    square = (states, states)
    count = 48 + 16 * (panels - 1)
    combine = 2 * states * states * width
    a, c, j, vecs = pl.pallas_call(
        functools.partial(kernel, panels, {}),
        out_shape=(panel, panel, panel, jax.ShapeDtypeStruct((2, 16, states), F32)),
        in_specs=[vmem] * 7,
        out_specs=(anywhere,) * 3 + (vmem,),
        scratch_shapes=[
            pltpu.VMEM((2,) + square, BF16),
            pltpu.VMEM((2,) + square, BF16),
            pltpu.VMEM((4,) + square, BF16),
            pltpu.VMEM((2,) + square, BF16),
            pltpu.VMEM((2, 2, 16, states), F32),
            pltpu.VMEM((2, 2, 16, states), F32),
            pltpu.VMEM((states, width), BF16),
            pltpu.VMEM((states, width), BF16),
            pltpu.VMEM((states, width), BF16),
            pltpu.VMEM((states, width), BF16),
            pltpu.SemaphoreType.DMA((count,)),
            pltpu.SemaphoreType.DMA((count,)),
            pltpu.SemaphoreType.DMA((count,)),
        ],
        compiler_params=pltpu.CompilerParams(
            collective_id=0, has_side_effects=True, vmem_limit_bytes=56 * 2**20
        ),
        cost_estimate=pl.CostEstimate(
            flops=18 * combine, bytes_accessed=12 * states * width, transcendentals=0
        ),
    )(
        transition[0], spread[0], precision[0], drift, belief, probe_hosts, probe_values
    )
    row = jax.ShapeDtypeStruct((1, states), BF16)
    a, b, c, eta, j = pl.pallas_call(
        place,
        out_shape=(panel, row, panel, row, panel),
        in_specs=[anywhere] * 3 + [vmem],
        out_specs=(anywhere, vmem, anywhere, vmem, anywhere),
        scratch_shapes=[
            pltpu.VMEM((3, 2, states // 2, width), BF16),
            pltpu.SemaphoreType.DMA((2, 3, 2)),
        ],
        cost_estimate=pl.CostEstimate(
            flops=0, bytes_accessed=12 * states * width, transcendentals=0
        ),
    )(a, c, j, vecs)
    return a[None], b, c[None], eta, j[None]


def solution(mesh):
    matrix = P("tm", None, "panel")
    vector = P("tm", None)
    return jax.shard_map(
        functools.partial(local, mesh.shape["panel"]),
        mesh=mesh,
        in_specs=(matrix, vector, matrix, vector, matrix, vector, vector),
        out_specs=(matrix, vector, matrix, vector, matrix),
        check_vma=False,
    )
```

```python
import functools

import jax
import jax.numpy as jnp
from jax import lax
from jax.experimental import pallas as pl
from jax.experimental.pallas import tpu as pltpu
from jax.sharding import PartitionSpec as P

NS = 2
TERMS = 2**NS - 1
F32 = jnp.float32
BF16 = jnp.bfloat16
MESH = pl.DeviceIdType.MESH
NN = (((1,), (0,)), ((), ()))
NT = (((1,), (1,)), ((), ()))
TN = (((0,), (0,)), ((), ()))


def dot(lhs, rhs, dims=NN):
    return lax.dot_general(lhs, rhs, dims, preferred_element_type=F32)


def kernel(
    panels, names,
    a_ref, c_ref, j_ref, b_ref, eta_ref, hosts_ref, values_ref,
    a_out, c_out, j_out, vec_out,
    s0, a0, s1, a1, p0, p1, v0, v1, anchor, cur, inner, weighted, send_sem, recv_sem, place_sem,
):
    states, width = a_ref.shape
    tile = min(width, 256)
    tiles = width // tile
    time = lax.axis_index("tm")
    me = lax.axis_index("panel")
    core = lax.rem(time, 2)
    half = lax.rem(lax.div(time, 2), 2)
    core_peer = time + 1 - 2 * core
    side_peer = time + 2 - 4 * half
    cross_peer = core_peer + 2 - 4 * half
    own_cols = pl.ds(pl.multiple_of(me * width, width), width)

    def sem(name):
        return names.setdefault(name, len(names))

    def copy(name, src, dst, at, panel=None):
        index = sem(name)
        return pltpu.make_async_remote_copy(
            src_ref=src, dst_ref=dst,
            send_sem=send_sem.at[index], recv_sem=recv_sem.at[index],
            device_id=(at, me if panel is None else panel), device_id_type=MESH,
        )

    def panel_block(ref, slot, rows, cols):
        return ref.at[slot, rows, cols]

    def chunk_rows(target, chunk):
        if panels != 2:
            return pl.ds(0, states)
        block = lax.rem(target + chunk, 2)
        return pl.ds(pl.multiple_of(block * width, width), width)

    def cols_of(panel):
        return pl.ds(pl.multiple_of(panel * width, width), width)

    def across(name, ref, slot, step, chunk):
        target = lax.rem(me + step, panels)
        block = panel_block(ref, slot, chunk_rows(target, chunk), own_cols)
        return copy(f"{name}y{step}.{chunk}", block, block, time, target)

    def onward(name, ref, slot, step, chunk):
        source = lax.rem(me - step + panels, panels)
        block = panel_block(ref, slot, chunk_rows(me, chunk), cols_of(source))
        return copy(f"{name}f{step}.{chunk}", block, block, core_peer)

    def beside(name, ref, slot, chunk):
        block = panel_block(ref, slot, chunk_rows(me + 1, chunk), own_cols)
        return copy(f"{name}c{chunk}", block, block, core_peer)

    def sideways(name, ref, slot, chunk, at=side_peer):
        block = panel_block(ref, slot, chunk_rows(me + 1, chunk), own_cols)
        return copy(f"{name}x{chunk}", block, block, at)

    steps = range(1, panels)
    sym_chunks = (1,) if panels == 2 else (0,)
    all_chunks = (0, 1) if panels == 2 else (0,)
    sym_first = all_chunks[::-1]

    def products(lhs, rhs, dims, put):
        for index in range(tiles):
            cols = pl.ds(index * tile, tile)
            put(cols, dot(lhs[...], rhs(cols), dims))

    def into(ref):
        def put(cols, value):
            ref[:, cols] = value.astype(BF16)
        return put

    strip = states // 4
    strips = 2

    def half_product(name, both, index):
        cols = pl.ds(pl.multiple_of(core * (strips * strip) + index * strip, strip), strip)
        return cols, copy(f"{name}p{index}", both.at[:, cols], both.at[:, cols], core_peer)

    def form_both(name, cov, info, both):
        for index in range(strips):
            cols, send = half_product(name, both, index)
            both[:, cols] = dot(cov[...], info[:, cols]).astype(BF16)
            send.start()
        for index in range(strips):
            half_product(name, both, index)[1].wait_recv()

    def end_both(name, both):
        for index in range(strips):
            half_product(name, both, index)[1].wait_send()

    def series(both):
        cur[...] = anchor[...]

        @pl.loop(0, TERMS)
        def _(repeat):
            def put(cols, value):
                cur[:, cols] = (anchor[:, cols].astype(F32) - value).astype(BF16)

            products(both, lambda cols: cur[:, cols], NN, put)

    def vec_series(start, both, dims):
        def step(repeat, vector):
            return start - dot(vector.astype(BF16), both[...], dims)

        return lax.fori_loop(0, TERMS, step, start)

    def mirror(ref, slot):
        if panels == 2:
            other = pl.ds(pl.multiple_of((1 - me) * width, width), width)
            ref[slot, own_cols, other] = ref[slot, other, own_cols].T

    def start_across(name, ref, slot, chunks):
        for step in steps:
            for chunk in chunks:
                across(name, ref, slot, step, chunk).start()

    def start_beside(name, ref, slot, chunks=sym_first):
        for chunk in chunks:
            beside(name, ref, slot, chunk).start()

    def pass_sym(name, ref, slot):
        for step in steps:
            for chunk in sym_chunks:
                across(name, ref, slot, step, chunk).wait_recv()
                onward(name, ref, slot, step, chunk).start()

    def gather_sym(name, ref, slot):
        for chunk in sym_first:
            beside(name, ref, slot, chunk).wait_recv()
        for step in steps:
            for chunk in sym_chunks:
                onward(name, ref, slot, step, chunk).wait_recv()
        mirror(ref, 0)
        mirror(ref, 1)

    def end_sends(name, ref, slot):
        for step in steps:
            for chunk in sym_chunks:
                if name != "s0":
                    across(name, ref, slot, step, chunk).wait_send()
                onward(name, ref, slot, step, chunk).wait_send()
        for chunk in sym_first:
            beside(name, ref, slot, chunk).wait_send()

    def keep(name, src, dst, index):
        cols = pl.ds(index * tile, tile)
        return pltpu.make_async_copy(
            src.at[:, cols], dst.at[:, cols], place_sem.at[sem(f"{name}{index}")]
        )

    def share(name, src, dst, index):
        cols = pl.ds(index * tile, tile)
        return copy(f"{name}{index}", src.at[:, cols], dst.at[:, cols], core_peer)

    def start_result(name, src, dst, cols):
        share(name, src, dst, cols.start // tile).start()
        keep(name, src, dst, cols.start // tile).start()

    def end_results(name, src, dst):
        for index in range(tiles):
            keep(name, src, dst, index).wait()
            share(name, src, dst, index).wait_send()

    def end_arrivals(name, src, dst):
        for index in range(tiles):
            share(name, src, dst, index).wait_recv()

    barrier = pltpu.get_barrier_semaphore()
    for at in (core_peer, side_peer, cross_peer):
        pl.semaphore_signal(barrier, inc=1, device_id=(at, me), device_id_type=MESH)
    for step in steps:
        pl.semaphore_signal(
            barrier, inc=1, device_id=(time, lax.rem(me + step, panels)), device_id_type=MESH
        )
    pl.semaphore_wait(barrier, 3 + len(steps))

    @pl.when(core == 0)
    def _():
        s0[0, :, own_cols] = c_ref[...]

    @pl.when(core == 1)
    def _():
        s0[1, :, own_cols] = j_ref[...]

    start_across("s0", s0, core, sym_chunks)
    start_beside("s0", s0, core)
    a0[core, :, own_cols] = a_ref[...]

    @pl.when(core == 1)
    def _():
        start_beside("a0", a0, 1, all_chunks)

    hosts = jnp.broadcast_to(hosts_ref[...].astype(F32) * 2.0, (8, hosts_ref.shape[1])).T[:, :1]
    values = jnp.broadcast_to(values_ref[...], (8, values_ref.shape[1])).T[:, :1]
    spots = lax.broadcasted_iota(jnp.int32, (hosts.shape[0], states), 1).astype(F32)
    paired = jnp.sum(jnp.where(hosts == spots, values, 0.0), axis=0, keepdims=True)
    belief = (eta_ref[...].astype(F32) + paired).astype(BF16).astype(F32)
    v0[core, 0] = jnp.broadcast_to(b_ref[...].astype(F32), (16, states))
    v0[core, 1] = jnp.broadcast_to(belief, (16, states))

    def vec0():
        return copy("v0", v0.at[core], v0.at[core], core_peer)

    vec0().start()
    for step in steps:
        for chunk in sym_chunks:
            across("s0", s0, core, step, chunk).wait_send()
    start_across("a0", a0, core, all_chunks)
    pass_sym("s0", s0, core)
    gather_sym("s0", s0, core)
    form_both("p0", s0.at[0], s0.at[1], p0)
    vec0().wait_recv()

    def vec1(kind, at, tag):
        block = v1.at[half, kind]
        return copy(f"v1{kind}{tag}", block, block, at)

    vec1_peers = ((core_peer, "c"), (side_peer, "x"), (cross_peer, "d"))

    def take_move(chunks):
        for chunk in chunks:
            sideways("a1", a1, 1, chunk).wait_recv()
            start_across("a1", a1, 1, (chunk,))
            beside("b1", a1, 1, chunk).start()

    def late_part(name, cov, both, moves, vecs, addend, ready, store):
        start = vecs[0, 0] + dot(vecs[1, 1].astype(BF16), cov[...])
        forward = vec_series(start, both, NT)
        if name == "a1":
            @pl.when(half == 0)
            def _():
                take_move(all_chunks[1:])

        for step in steps:
            across(name, moves, 1, step, 0).wait_recv()
        for step in steps:
            onward(name, moves, 1, step, 0).start()
        own_rows = me * width

        def rows(cols):
            return moves[1, pl.ds(pl.multiple_of(own_rows + cols.start, tile), tile), :]

        products(cov, rows, NT, into(anchor))
        series(both)
        for step in steps:
            for chunk in all_chunks[1:]:
                across(name, moves, 1, step, chunk).wait_recv()
                onward(name, moves, 1, step, chunk).start()

        ready()

        def put(cols, value):
            store(cols, (value + addend(cols).astype(F32)).astype(BF16))

        products(moves.at[1], lambda cols: cur[:, cols], NN, put)
        fresh = dot(forward.astype(BF16), moves[1], NT) + vecs[1, 0]
        return fresh.astype(BF16).astype(F32)

    def early_part(name, info, both, moves, vecs, addend, ready_info, store_info, sent_info, store_move):
        def vector():
            start = vecs[1, 1] - dot(vecs[0, 0].astype(BF16), info[...])
            return vec_series(start, both, NN)

        anchor[...] = moves[0, :, own_cols]
        series(both)
        products(info, lambda cols: cur[:, cols], NN, into(weighted))
        backward = vector()
        for step in steps:
            for chunk in all_chunks:
                across(name, moves, 0, step, chunk).wait_recv()

        ready_info()

        def put(cols, value):
            store_info(cols, (value + addend(cols).astype(F32)).astype(BF16))

        products(moves.at[0], lambda cols: weighted[:, cols], TN, put)
        sent_info()
        fresh = dot(backward.astype(BF16), moves[0]) + vecs[0, 1]
        if name == "a0":
            for chunk in all_chunks:
                beside(name, moves, 1, chunk).wait_recv()
        else:
            @pl.when(half == 0)
            def _():
                for chunk in all_chunks:
                    beside("b1", moves, 1, chunk).wait_recv()

        for step in steps:
            for chunk in all_chunks:
                onward(name, moves, 1, step, chunk).wait_recv()
        products(moves.at[1], lambda cols: cur[:, cols], NN, store_move)
        return fresh.astype(BF16).astype(F32)

    info_slot = 2 - half
    cov_slot = 3 * half

    def wide(cols):
        return pl.ds(pl.multiple_of(me * width + cols.start, tile), tile)

    def share_vec(kind, value):
        v1[half, kind] = value
        for at, tag in vec1_peers:
            vec1(kind, at, tag).start()

    @pl.when(core == 0)
    def _():
        def store_info(cols, value):
            s1[info_slot, :, wide(cols)] = value

        def store_move(cols, value):
            a1[half, :, wide(cols)] = value.astype(BF16)

        def sent_info():
            @pl.when(half == 1)
            def _():
                sideways("j1", s1, 1, sym_first[0]).start()
                start_across("s1", s1, 1, sym_chunks)
                start_beside("s1", s1, 1)

        fresh = early_part(
            "a0", s0.at[1], p0, a0, v0, lambda cols: j_ref[:, cols],
            lambda: None, store_info, sent_info, store_move,
        )
        share_vec(1, fresh)

        @pl.when(half == 0)
        def _():
            for chunk in all_chunks:
                sideways("a1", a1, 0, chunk).start()
            start_across("a1", a1, 0, all_chunks[:1])
            sideways("j1", s1, 1, sym_first[0]).wait_recv()
            start_across("s1", s1, 1, sym_chunks)
            start_beside("s1", s1, 1, sym_first[:1])

        @pl.when(half == 1)
        def _():
            start_beside("a1", a1, 1, all_chunks)
            sideways("j1", s1, 1, sym_first[0]).wait_send()
            for chunk in sym_first[1:]:
                sideways("j1", s1, 1, chunk).start()
            sideways("a1", a1, 1, 0, cross_peer).start()

        pass_sym("s1", s1, 1)

        @pl.when(half == 0)
        def _():
            for chunk in sym_first[1:]:
                sideways("j1", s1, 1, chunk).wait_recv()
                start_beside("s1", s1, 1, (chunk,))
            start_across("a1", a1, 0, all_chunks[1:])

        @pl.when(half == 1)
        def _():
            for chunk in all_chunks[1:]:
                sideways("j1", s1, 1, sym_first[1]).wait_send()
                sideways("a1", a1, 1, chunk, cross_peer).start()
            for chunk in all_chunks:
                sideways("a1", a1, 0, chunk).wait_recv()
                start_across("a1", a1, 0, (chunk,))

        gather_sym("s1", s1, 1)
        form_both("p1", s1.at[0], s1.at[1], p1)
        for kind, at, tag in ((0, core_peer, "c"), (1, side_peer, "x"), (0, cross_peer, "d")):
            vec1(kind, at, tag).wait_recv()

        @pl.when(half == 0)
        def _():
            for chunk in all_chunks:
                sideways("j1", s1, 2, chunk).start()

        def late_info():
            @pl.when(half == 1)
            def _():
                for chunk in all_chunks:
                    sideways("j1", s1, 2, chunk).wait_recv()

        def put_info(cols, value):
            inner[:, cols] = value
            start_result("jo", inner, j_out, cols)

        def put_move(cols, value):
            anchor[:, cols] = value.astype(BF16)
            start_result("ao", anchor, a_out, cols)

        fresh = early_part(
            "a1", s1.at[1], p1, a1, v1, lambda cols: s1[2, :, wide(cols)],
            late_info, put_info, lambda: None, put_move,
        )
        vec_out[1] = fresh
        copy("eo", vec_out.at[1], vec_out.at[1], core_peer).start()
        end_arrivals("co", weighted, c_out)
        copy("bo", vec_out.at[0], vec_out.at[0], core_peer).wait_recv()
        for step in steps:
            for chunk in all_chunks:
                across("a0", a0, 0, step, chunk).wait_send()
                across("a1", a1, 0, step, chunk).wait_send()
        end_sends("s1", s1, 1)

        @pl.when(half == 0)
        def _():
            for chunk in all_chunks:
                sideways("j1", s1, 2, chunk).wait_send()
                sideways("a1", a1, 0, chunk).wait_send()

        @pl.when(half == 1)
        def _():
            for chunk in all_chunks:
                sideways("a1", a1, 1, chunk, cross_peer).wait_send()
                beside("a1", a1, 1, chunk).wait_send()

        for at, tag in vec1_peers:
            vec1(1, at, tag).wait_send()
        end_results("jo", inner, j_out)
        end_results("ao", anchor, a_out)
        copy("eo", vec_out.at[1], vec_out.at[1], core_peer).wait_send()

    @pl.when(core == 1)
    def _():
        def store_cov(cols, value):
            s1[cov_slot, :, wide(cols)] = value

        fresh = late_part(
            "a0", s0.at[0], p0, a0, v0, lambda cols: c_ref[:, cols],
            lambda: None, store_cov
        )

        @pl.when(half == 0)
        def _():
            start_across("s1", s1, 0, sym_chunks)
            for chunk in sym_first:
                sideways("c1", s1, 0, chunk).start()
            start_beside("s1", s1, 0)

        share_vec(0, fresh)

        @pl.when(half == 1)
        def _():
            for chunk in all_chunks:
                beside("a1", a1, 1, chunk).wait_recv()
            start_across("a1", a1, 1, all_chunks[:1])
            sideways("c1", s1, 0, sym_first[0]).wait_recv()
            start_across("s1", s1, 0, sym_chunks)
            start_beside("s1", s1, 0, sym_first[:1])

        pass_sym("s1", s1, 0)

        @pl.when(half == 1)
        def _():
            for chunk in sym_first[1:]:
                sideways("c1", s1, 0, chunk).wait_recv()
                start_beside("s1", s1, 0, (chunk,))
            start_across("a1", a1, 1, all_chunks[1:])
            for chunk in all_chunks:
                sideways("c1", s1, 3, chunk).start()

        @pl.when(half == 0)
        def _():
            take_move(all_chunks[:1])

        gather_sym("s1", s1, 0)
        form_both("p1", s1.at[0], s1.at[1], p1)
        for kind, at, tag in ((1, core_peer, "c"), (0, side_peer, "x"), (1, cross_peer, "d")):
            vec1(kind, at, tag).wait_recv()

        def late_cov():
            @pl.when(half == 0)
            def _():
                for chunk in all_chunks:
                    sideways("c1", s1, 3, chunk).wait_recv()

        def put_cov(cols, value):
            weighted[:, cols] = value
            start_result("co", weighted, c_out, cols)

        fresh = late_part(
            "a1", s1.at[0], p1, a1, v1, lambda cols: s1[3, :, wide(cols)],
            late_cov, put_cov
        )
        vec_out[0] = fresh
        copy("bo", vec_out.at[0], vec_out.at[0], core_peer).start()
        end_arrivals("jo", inner, j_out)
        end_arrivals("ao", anchor, a_out)
        copy("eo", vec_out.at[1], vec_out.at[1], core_peer).wait_recv()
        for step in steps:
            for chunk in all_chunks:
                for name, ref in (("a0", a0), ("a1", a1)):
                    across(name, ref, 1, step, chunk).wait_send()
                    onward(name, ref, 1, step, chunk).wait_send()
        for chunk in all_chunks:
            beside("a0", a0, 1, chunk).wait_send()
            sideways("c1", s1, cov_slot, chunk).wait_send()

        @pl.when(half == 0)
        def _():
            for chunk in all_chunks:
                beside("b1", a1, 1, chunk).wait_send()

        end_sends("s1", s1, 0)
        for at, tag in vec1_peers:
            vec1(0, at, tag).wait_send()
        end_results("co", weighted, c_out)
        copy("bo", vec_out.at[0], vec_out.at[0], core_peer).wait_send()

    end_both("p0", p0)
    end_both("p1", p1)
    end_sends("s0", s0, core)
    vec0().wait_send()


def place(a_ref, c_ref, j_ref, vec_ref, a_out, b_out, c_out, eta_out, j_out, held, sems):
    pieces = held.shape[1]
    rows = held.shape[2]
    fetches, sends = [], []
    for index, (src, dst) in enumerate(((a_ref, a_out), (c_ref, c_out), (j_ref, j_out))):
        for piece in range(pieces):
            block = pl.ds(piece * rows, rows)
            slot = held.at[index, piece]
            fetches.append(pltpu.make_async_copy(src.at[block], slot, sems.at[0, index, piece]))
            sends.append(pltpu.make_async_copy(slot, dst.at[block], sems.at[1, index, piece]))
    for fetch in fetches:
        fetch.start()
    b_out[...] = vec_ref[0, 0:1].astype(BF16)
    eta_out[...] = vec_ref[1, 0:1].astype(BF16)
    for fetch, send in zip(fetches, sends):
        fetch.wait()
        send.start()
    for send in sends:
        send.wait()


def local(panels, transition, drift, spread, belief, precision, probe_hosts, probe_values):
    states, width = transition.shape[1:]
    panel = jax.ShapeDtypeStruct((states, width), BF16)
    vmem = pl.BlockSpec(memory_space=pltpu.VMEM)
    anywhere = pl.BlockSpec(memory_space=pl.ANY)
    square = (states, states)
    count = 48 + 16 * (panels - 1)
    combine = 2 * states * states * width
    a, c, j, vecs = pl.pallas_call(
        functools.partial(kernel, panels, {}),
        out_shape=(panel, panel, panel, jax.ShapeDtypeStruct((2, 16, states), F32)),
        in_specs=[vmem] * 7,
        out_specs=(anywhere,) * 3 + (vmem,),
        scratch_shapes=[
            pltpu.VMEM((2,) + square, BF16),
            pltpu.VMEM((2,) + square, BF16),
            pltpu.VMEM((4,) + square, BF16),
            pltpu.VMEM((2,) + square, BF16),
            pltpu.VMEM(square, BF16),
            pltpu.VMEM(square, BF16),
            pltpu.VMEM((2, 2, 16, states), F32),
            pltpu.VMEM((2, 2, 16, states), F32),
            pltpu.VMEM((states, width), BF16),
            pltpu.VMEM((states, width), BF16),
            pltpu.VMEM((states, width), BF16),
            pltpu.VMEM((states, width), BF16),
            pltpu.SemaphoreType.DMA((count,)),
            pltpu.SemaphoreType.DMA((count,)),
            pltpu.SemaphoreType.DMA((count,)),
        ],
        compiler_params=pltpu.CompilerParams(
            collective_id=0, has_side_effects=True, vmem_limit_bytes=56 * 2**20
        ),
        cost_estimate=pl.CostEstimate(
            flops=18 * combine, bytes_accessed=12 * states * width, transcendentals=0
        ),
    )(
        transition[0], spread[0], precision[0], drift, belief, probe_hosts, probe_values
    )
    row = jax.ShapeDtypeStruct((1, states), BF16)
    a, b, c, eta, j = pl.pallas_call(
        place,
        out_shape=(panel, row, panel, row, panel),
        in_specs=[anywhere] * 3 + [vmem],
        out_specs=(anywhere, vmem, anywhere, vmem, anywhere),
        scratch_shapes=[
            pltpu.VMEM((3, 2, states // 2, width), BF16),
            pltpu.SemaphoreType.DMA((2, 3, 2)),
        ],
        cost_estimate=pl.CostEstimate(
            flops=0, bytes_accessed=12 * states * width, transcendentals=0
        ),
    )(a, c, j, vecs)
    return a[None], b, c[None], eta, j[None]


def solution(mesh):
    matrix = P("tm", None, "panel")
    vector = P("tm", None)
    return jax.shard_map(
        functools.partial(local, mesh.shape["panel"]),
        mesh=mesh,
        in_specs=(matrix, vector, matrix, vector, matrix, vector, vector),
        out_specs=(matrix, vector, matrix, vector, matrix),
        check_vma=False,
    )
```

```python
import functools

import jax
import jax.numpy as jnp
from jax import lax
from jax.experimental import pallas as pl
from jax.experimental.pallas import tpu as pltpu
from jax.sharding import PartitionSpec as P

NS = 2
TERMS = 2**NS - 1
F32 = jnp.float32
BF16 = jnp.bfloat16
MESH = pl.DeviceIdType.MESH
NN = (((1,), (0,)), ((), ()))
NT = (((1,), (1,)), ((), ()))
TN = (((0,), (0,)), ((), ()))


def dot(lhs, rhs, dims=NN):
    return lax.dot_general(lhs, rhs, dims, preferred_element_type=F32)


def kernel(
    panels, names,
    a_ref, c_ref, j_ref, b_ref, eta_ref, hosts_ref, values_ref,
    a_out, c_out, j_out, vec_out,
    s0, a0, s1, a1, v0, v1, anchor, cur, inner, weighted, send_sem, recv_sem, place_sem,
):
    states, width = a_ref.shape
    tile = min(width, 256)
    tiles = width // tile
    time = lax.axis_index("tm")
    me = lax.axis_index("panel")
    core = lax.rem(time, 2)
    half = lax.rem(lax.div(time, 2), 2)
    core_peer = time + 1 - 2 * core
    side_peer = time + 2 - 4 * half
    cross_peer = core_peer + 2 - 4 * half
    own_cols = pl.ds(pl.multiple_of(me * width, width), width)

    def sem(name):
        return names.setdefault(name, len(names))

    def copy(name, src, dst, at, panel=None):
        index = sem(name)
        return pltpu.make_async_remote_copy(
            src_ref=src, dst_ref=dst,
            send_sem=send_sem.at[index], recv_sem=recv_sem.at[index],
            device_id=(at, me if panel is None else panel), device_id_type=MESH,
        )

    def panel_block(ref, slot, rows, cols):
        return ref.at[slot, rows, cols]

    def chunk_rows(target, chunk):
        if panels != 2:
            return pl.ds(0, states)
        block = lax.rem(target + chunk, 2)
        return pl.ds(pl.multiple_of(block * width, width), width)

    def cols_of(panel):
        return pl.ds(pl.multiple_of(panel * width, width), width)

    def across(name, ref, slot, step, chunk):
        target = lax.rem(me + step, panels)
        block = panel_block(ref, slot, chunk_rows(target, chunk), own_cols)
        return copy(f"{name}y{step}.{chunk}", block, block, time, target)

    def onward(name, ref, slot, step, chunk):
        source = lax.rem(me - step + panels, panels)
        block = panel_block(ref, slot, chunk_rows(me, chunk), cols_of(source))
        return copy(f"{name}f{step}.{chunk}", block, block, core_peer)

    def beside(name, ref, slot, chunk):
        block = panel_block(ref, slot, chunk_rows(me + 1, chunk), own_cols)
        return copy(f"{name}c{chunk}", block, block, core_peer)

    def sideways(name, ref, slot, chunk, at=side_peer):
        block = panel_block(ref, slot, chunk_rows(me + 1, chunk), own_cols)
        return copy(f"{name}x{chunk}", block, block, at)

    steps = range(1, panels)
    sym_chunks = (1,) if panels == 2 else (0,)
    all_chunks = (0, 1) if panels == 2 else (0,)
    sym_first = all_chunks[::-1]

    def products(lhs, rhs, dims, put):
        for index in range(tiles):
            cols = pl.ds(index * tile, tile)
            put(cols, dot(lhs[...], rhs(cols), dims))

    def into(ref):
        def put(cols, value):
            ref[:, cols] = value.astype(BF16)
        return put

    def series(cov, info):
        cur[...] = anchor[...]

        @pl.loop(0, TERMS)
        def _(repeat):
            products(info, lambda cols: cur[:, cols], NN, into(inner))

            def put(cols, value):
                cur[:, cols] = (anchor[:, cols].astype(F32) - value).astype(BF16)

            products(cov, lambda cols: inner[:, cols], NN, put)

    def vec_series(start, first, second):
        def step(repeat, vector):
            middle = dot(vector.astype(BF16), first[...])
            return start - dot(middle.astype(BF16), second[...])

        return lax.fori_loop(0, TERMS, step, start)

    def mirror(ref, slot):
        if panels == 2:
            other = pl.ds(pl.multiple_of((1 - me) * width, width), width)
            ref[slot, own_cols, other] = ref[slot, other, own_cols].T

    def start_across(name, ref, slot, chunks):
        for step in steps:
            for chunk in chunks:
                across(name, ref, slot, step, chunk).start()

    def start_beside(name, ref, slot, chunks=sym_first):
        for chunk in chunks:
            beside(name, ref, slot, chunk).start()

    def pass_sym(name, ref, slot):
        for step in steps:
            for chunk in sym_chunks:
                across(name, ref, slot, step, chunk).wait_recv()
                onward(name, ref, slot, step, chunk).start()

    def gather_sym(name, ref, slot):
        for chunk in sym_first:
            beside(name, ref, slot, chunk).wait_recv()
        for step in steps:
            for chunk in sym_chunks:
                onward(name, ref, slot, step, chunk).wait_recv()
        mirror(ref, 0)
        mirror(ref, 1)

    def end_sends(name, ref, slot):
        for step in steps:
            for chunk in sym_chunks:
                if name != "s0":
                    across(name, ref, slot, step, chunk).wait_send()
                onward(name, ref, slot, step, chunk).wait_send()
        for chunk in sym_first:
            beside(name, ref, slot, chunk).wait_send()

    def keep(name, src, dst, index):
        cols = pl.ds(index * tile, tile)
        return pltpu.make_async_copy(
            src.at[:, cols], dst.at[:, cols], place_sem.at[sem(f"{name}{index}")]
        )

    def share(name, src, dst, index):
        cols = pl.ds(index * tile, tile)
        return copy(f"{name}{index}", src.at[:, cols], dst.at[:, cols], core_peer)

    def start_result(name, src, dst, cols):
        share(name, src, dst, cols.start // tile).start()
        keep(name, src, dst, cols.start // tile).start()

    def end_results(name, src, dst):
        for index in range(tiles):
            keep(name, src, dst, index).wait()
            share(name, src, dst, index).wait_send()

    def end_arrivals(name, src, dst):
        for index in range(tiles):
            share(name, src, dst, index).wait_recv()

    barrier = pltpu.get_barrier_semaphore()
    for at in (core_peer, side_peer, cross_peer):
        pl.semaphore_signal(barrier, inc=1, device_id=(at, me), device_id_type=MESH)
    for step in steps:
        pl.semaphore_signal(
            barrier, inc=1, device_id=(time, lax.rem(me + step, panels)), device_id_type=MESH
        )
    pl.semaphore_wait(barrier, 3 + len(steps))

    @pl.when(core == 0)
    def _():
        s0[0, :, own_cols] = c_ref[...]

    @pl.when(core == 1)
    def _():
        s0[1, :, own_cols] = j_ref[...]

    start_across("s0", s0, core, sym_chunks)
    start_beside("s0", s0, core)
    a0[core, :, own_cols] = a_ref[...]

    @pl.when(core == 1)
    def _():
        start_across("a0", a0, 1, all_chunks[:1])
        start_beside("a0", a0, 1, all_chunks)

    hosts = jnp.broadcast_to(hosts_ref[...].astype(F32) * 2.0, (8, hosts_ref.shape[1])).T[:, :1]
    values = jnp.broadcast_to(values_ref[...], (8, values_ref.shape[1])).T[:, :1]
    spots = lax.broadcasted_iota(jnp.int32, (hosts.shape[0], states), 1).astype(F32)
    paired = jnp.sum(jnp.where(hosts == spots, values, 0.0), axis=0, keepdims=True)
    belief = (eta_ref[...].astype(F32) + paired).astype(BF16).astype(F32)
    v0[core, 0] = jnp.broadcast_to(b_ref[...].astype(F32), (16, states))
    v0[core, 1] = jnp.broadcast_to(belief, (16, states))

    def vec0():
        return copy("v0", v0.at[core], v0.at[core], core_peer)

    vec0().start()
    for step in steps:
        for chunk in sym_chunks:
            across("s0", s0, core, step, chunk).wait_send()

    @pl.when(core == 0)
    def _():
        start_across("a0", a0, 0, all_chunks)

    @pl.when(core == 1)
    def _():
        start_across("a0", a0, 1, all_chunks[1:])

    pass_sym("s0", s0, core)
    gather_sym("s0", s0, core)
    vec0().wait_recv()

    def vec1(kind, at, tag):
        block = v1.at[half, kind]
        return copy(f"v1{kind}{tag}", block, block, at)

    vec1_peers = ((core_peer, "c"), (side_peer, "x"), (cross_peer, "d"))

    def take_move(chunks):
        for chunk in chunks:
            sideways("a1", a1, 1, chunk).wait_recv()
            start_across("a1", a1, 1, (chunk,))
            beside("b1", a1, 1, chunk).start()

    def late_part(name, cov, info, moves, vecs, addend, ready, store):
        start = vecs[0, 0] + dot(vecs[1, 1].astype(BF16), cov[...])
        forward = vec_series(start, info, cov)
        if name == "a1":
            @pl.when(half == 0)
            def _():
                take_move(all_chunks[1:])

        for step in steps:
            across(name, moves, 1, step, 0).wait_recv()
        for step in steps:
            onward(name, moves, 1, step, 0).start()
        own_rows = me * width

        def rows(cols):
            return moves[1, pl.ds(pl.multiple_of(own_rows + cols.start, tile), tile), :]

        products(cov, rows, NT, into(anchor))
        series(cov, info)
        for step in steps:
            for chunk in all_chunks[1:]:
                across(name, moves, 1, step, chunk).wait_recv()
                onward(name, moves, 1, step, chunk).start()

        ready()

        def put(cols, value):
            store(cols, (value + addend(cols).astype(F32)).astype(BF16))

        products(moves.at[1], lambda cols: cur[:, cols], NN, put)
        fresh = dot(forward.astype(BF16), moves[1], NT) + vecs[1, 0]
        return fresh.astype(BF16).astype(F32)

    def early_part(name, cov, info, moves, vecs, addend, ready_info, store_info, sent_info, store_move):
        def vector():
            start = vecs[1, 1] - dot(vecs[0, 0].astype(BF16), info[...])
            return vec_series(start, cov, info)

        anchor[...] = moves[0, :, own_cols]
        series(cov, info)
        products(info, lambda cols: cur[:, cols], NN, into(weighted))
        backward = vector()
        for step in steps:
            for chunk in all_chunks:
                across(name, moves, 0, step, chunk).wait_recv()

        ready_info()

        def put(cols, value):
            store_info(cols, (value + addend(cols).astype(F32)).astype(BF16))

        products(moves.at[0], lambda cols: weighted[:, cols], TN, put)
        sent_info()
        fresh = dot(backward.astype(BF16), moves[0]) + vecs[0, 1]
        if name == "a0":
            for chunk in all_chunks:
                beside(name, moves, 1, chunk).wait_recv()
        else:
            @pl.when(half == 0)
            def _():
                for chunk in all_chunks:
                    beside("b1", moves, 1, chunk).wait_recv()

        for step in steps:
            for chunk in all_chunks:
                onward(name, moves, 1, step, chunk).wait_recv()
        products(moves.at[1], lambda cols: cur[:, cols], NN, store_move)
        return fresh.astype(BF16).astype(F32)

    info_slot = 2 - half
    cov_slot = 3 * half

    def wide(cols):
        return pl.ds(pl.multiple_of(me * width + cols.start, tile), tile)

    def share_vec(kind, value):
        v1[half, kind] = value
        for at, tag in vec1_peers:
            vec1(kind, at, tag).start()

    @pl.when(core == 0)
    def _():
        def store_info(cols, value):
            s1[info_slot, :, wide(cols)] = value

        def store_move(cols, value):
            a1[half, :, wide(cols)] = value.astype(BF16)

        def sent_info():
            @pl.when(half == 1)
            def _():
                sideways("j1", s1, 1, sym_first[0]).start()
                start_across("s1", s1, 1, sym_chunks)
                start_beside("s1", s1, 1)

        fresh = early_part(
            "a0", s0.at[0], s0.at[1], a0, v0, lambda cols: j_ref[:, cols],
            lambda: None, store_info, sent_info, store_move,
        )
        share_vec(1, fresh)

        @pl.when(half == 0)
        def _():
            for chunk in all_chunks:
                sideways("a1", a1, 0, chunk).start()
            start_across("a1", a1, 0, all_chunks[:1])
            sideways("j1", s1, 1, sym_first[0]).wait_recv()
            start_across("s1", s1, 1, sym_chunks)
            start_beside("s1", s1, 1, sym_first[:1])

        @pl.when(half == 1)
        def _():
            start_beside("a1", a1, 1, all_chunks)
            sideways("j1", s1, 1, sym_first[0]).wait_send()
            for chunk in sym_first[1:]:
                sideways("j1", s1, 1, chunk).start()
            sideways("a1", a1, 1, 0, cross_peer).start()

        pass_sym("s1", s1, 1)

        @pl.when(half == 0)
        def _():
            for chunk in sym_first[1:]:
                sideways("j1", s1, 1, chunk).wait_recv()
                start_beside("s1", s1, 1, (chunk,))
            start_across("a1", a1, 0, all_chunks[1:])

        @pl.when(half == 1)
        def _():
            for chunk in all_chunks[1:]:
                sideways("j1", s1, 1, sym_first[1]).wait_send()
                sideways("a1", a1, 1, chunk, cross_peer).start()
            for chunk in all_chunks:
                sideways("a1", a1, 0, chunk).wait_recv()
                start_across("a1", a1, 0, (chunk,))

        gather_sym("s1", s1, 1)
        for kind, at, tag in ((0, core_peer, "c"), (1, side_peer, "x"), (0, cross_peer, "d")):
            vec1(kind, at, tag).wait_recv()

        @pl.when(half == 0)
        def _():
            for chunk in all_chunks:
                sideways("j1", s1, 2, chunk).start()

        def late_info():
            @pl.when(half == 1)
            def _():
                for chunk in all_chunks:
                    sideways("j1", s1, 2, chunk).wait_recv()

        def put_info(cols, value):
            inner[:, cols] = value
            start_result("jo", inner, j_out, cols)

        def put_move(cols, value):
            anchor[:, cols] = value.astype(BF16)
            start_result("ao", anchor, a_out, cols)

        fresh = early_part(
            "a1", s1.at[0], s1.at[1], a1, v1, lambda cols: s1[2, :, wide(cols)],
            late_info, put_info, lambda: None, put_move,
        )
        vec_out[1] = fresh
        copy("eo", vec_out.at[1], vec_out.at[1], core_peer).start()
        end_arrivals("co", weighted, c_out)
        copy("bo", vec_out.at[0], vec_out.at[0], core_peer).wait_recv()
        for step in steps:
            for chunk in all_chunks:
                across("a0", a0, 0, step, chunk).wait_send()
                across("a1", a1, 0, step, chunk).wait_send()
        end_sends("s1", s1, 1)

        @pl.when(half == 0)
        def _():
            for chunk in all_chunks:
                sideways("j1", s1, 2, chunk).wait_send()
                sideways("a1", a1, 0, chunk).wait_send()

        @pl.when(half == 1)
        def _():
            for chunk in all_chunks:
                sideways("a1", a1, 1, chunk, cross_peer).wait_send()
                beside("a1", a1, 1, chunk).wait_send()

        for at, tag in vec1_peers:
            vec1(1, at, tag).wait_send()
        end_results("jo", inner, j_out)
        end_results("ao", anchor, a_out)
        copy("eo", vec_out.at[1], vec_out.at[1], core_peer).wait_send()

    @pl.when(core == 1)
    def _():
        def store_cov(cols, value):
            s1[cov_slot, :, wide(cols)] = value

        fresh = late_part(
            "a0", s0.at[0], s0.at[1], a0, v0, lambda cols: c_ref[:, cols],
            lambda: None, store_cov
        )

        @pl.when(half == 0)
        def _():
            start_across("s1", s1, 0, sym_chunks)
            for chunk in sym_first:
                sideways("c1", s1, 0, chunk).start()
            start_beside("s1", s1, 0)

        share_vec(0, fresh)

        @pl.when(half == 1)
        def _():
            for chunk in all_chunks:
                beside("a1", a1, 1, chunk).wait_recv()
            start_across("a1", a1, 1, all_chunks[:1])
            sideways("c1", s1, 0, sym_first[0]).wait_recv()
            start_across("s1", s1, 0, sym_chunks)
            start_beside("s1", s1, 0, sym_first[:1])

        pass_sym("s1", s1, 0)

        @pl.when(half == 1)
        def _():
            for chunk in sym_first[1:]:
                sideways("c1", s1, 0, chunk).wait_recv()
                start_beside("s1", s1, 0, (chunk,))
            start_across("a1", a1, 1, all_chunks[1:])
            for chunk in all_chunks:
                sideways("c1", s1, 3, chunk).start()

        @pl.when(half == 0)
        def _():
            take_move(all_chunks[:1])

        gather_sym("s1", s1, 0)
        for kind, at, tag in ((1, core_peer, "c"), (0, side_peer, "x"), (1, cross_peer, "d")):
            vec1(kind, at, tag).wait_recv()

        def late_cov():
            @pl.when(half == 0)
            def _():
                for chunk in all_chunks:
                    sideways("c1", s1, 3, chunk).wait_recv()

        def put_cov(cols, value):
            weighted[:, cols] = value
            start_result("co", weighted, c_out, cols)

        fresh = late_part(
            "a1", s1.at[0], s1.at[1], a1, v1, lambda cols: s1[3, :, wide(cols)],
            late_cov, put_cov
        )
        vec_out[0] = fresh
        copy("bo", vec_out.at[0], vec_out.at[0], core_peer).start()
        end_arrivals("jo", inner, j_out)
        end_arrivals("ao", anchor, a_out)
        copy("eo", vec_out.at[1], vec_out.at[1], core_peer).wait_recv()
        for step in steps:
            for chunk in all_chunks:
                for name, ref in (("a0", a0), ("a1", a1)):
                    across(name, ref, 1, step, chunk).wait_send()
                    onward(name, ref, 1, step, chunk).wait_send()
        for chunk in all_chunks:
            beside("a0", a0, 1, chunk).wait_send()
            sideways("c1", s1, cov_slot, chunk).wait_send()

        @pl.when(half == 0)
        def _():
            for chunk in all_chunks:
                beside("b1", a1, 1, chunk).wait_send()

        end_sends("s1", s1, 0)
        for at, tag in vec1_peers:
            vec1(0, at, tag).wait_send()
        end_results("co", weighted, c_out)
        copy("bo", vec_out.at[0], vec_out.at[0], core_peer).wait_send()

    end_sends("s0", s0, core)
    vec0().wait_send()


def place(a_ref, c_ref, j_ref, vec_ref, a_out, b_out, c_out, eta_out, j_out, held, sems):
    pieces = held.shape[1]
    rows = held.shape[2]
    fetches, sends = [], []
    for index, (src, dst) in enumerate(((a_ref, a_out), (c_ref, c_out), (j_ref, j_out))):
        for piece in range(pieces):
            block = pl.ds(piece * rows, rows)
            slot = held.at[index, piece]
            fetches.append(pltpu.make_async_copy(src.at[block], slot, sems.at[0, index, piece]))
            sends.append(pltpu.make_async_copy(slot, dst.at[block], sems.at[1, index, piece]))
    for fetch in fetches:
        fetch.start()
    b_out[...] = vec_ref[0, 0:1].astype(BF16)
    eta_out[...] = vec_ref[1, 0:1].astype(BF16)
    for fetch, send in zip(fetches, sends):
        fetch.wait()
        send.start()
    for send in sends:
        send.wait()


def local(panels, transition, drift, spread, belief, precision, probe_hosts, probe_values):
    states, width = transition.shape[1:]
    panel = jax.ShapeDtypeStruct((states, width), BF16)
    vmem = pl.BlockSpec(memory_space=pltpu.VMEM)
    anywhere = pl.BlockSpec(memory_space=pl.ANY)
    square = (states, states)
    count = 48 + 16 * (panels - 1)
    combine = 2 * states * states * width
    a, c, j, vecs = pl.pallas_call(
        functools.partial(kernel, panels, {}),
        out_shape=(panel, panel, panel, jax.ShapeDtypeStruct((2, 16, states), F32)),
        in_specs=[vmem] * 7,
        out_specs=(anywhere,) * 3 + (vmem,),
        scratch_shapes=[
            pltpu.VMEM((2,) + square, BF16),
            pltpu.VMEM((2,) + square, BF16),
            pltpu.VMEM((4,) + square, BF16),
            pltpu.VMEM((2,) + square, BF16),
            pltpu.VMEM((2, 2, 16, states), F32),
            pltpu.VMEM((2, 2, 16, states), F32),
            pltpu.VMEM((states, width), BF16),
            pltpu.VMEM((states, width), BF16),
            pltpu.VMEM((states, width), BF16),
            pltpu.VMEM((states, width), BF16),
            pltpu.SemaphoreType.DMA((count,)),
            pltpu.SemaphoreType.DMA((count,)),
            pltpu.SemaphoreType.DMA((count,)),
        ],
        compiler_params=pltpu.CompilerParams(
            collective_id=0, has_side_effects=True, vmem_limit_bytes=56 * 2**20
        ),
        cost_estimate=pl.CostEstimate(
            flops=18 * combine, bytes_accessed=12 * states * width, transcendentals=0
        ),
    )(
        transition[0], spread[0], precision[0], drift, belief, probe_hosts, probe_values
    )
    row = jax.ShapeDtypeStruct((1, states), BF16)
    a, b, c, eta, j = pl.pallas_call(
        place,
        out_shape=(panel, row, panel, row, panel),
        in_specs=[anywhere] * 3 + [vmem],
        out_specs=(anywhere, vmem, anywhere, vmem, anywhere),
        scratch_shapes=[
            pltpu.VMEM((3, 2, states // 2, width), BF16),
            pltpu.SemaphoreType.DMA((2, 3, 2)),
        ],
        cost_estimate=pl.CostEstimate(
            flops=0, bytes_accessed=12 * states * width, transcendentals=0
        ),
    )(a, c, j, vecs)
    return a[None], b, c[None], eta, j[None]


def solution(mesh):
    matrix = P("tm", None, "panel")
    vector = P("tm", None)
    return jax.shard_map(
        functools.partial(local, mesh.shape["panel"]),
        mesh=mesh,
        in_specs=(matrix, vector, matrix, vector, matrix, vector, vector),
        out_specs=(matrix, vector, matrix, vector, matrix),
        check_vma=False,
    )
```
